256 devices in a mesh: expert: 64 (over x, z_lo, y, core), dp: 4 (over z_hi).
Axes of the slice: x: 4, y: 4, z: 8 (z_hi: 4, z_lo: 2; z = z_hi * 2 + z_lo), core: 2. Of those that a mesh axis runs over, the one named last changes fastest.
Arguments:
- tokens: bfloat16 [4, 8192, 3584], P('dp', 'expert'), may hold values from -6 to 6
- routes: int32 [4, 8192, 2], P('dp', 'expert'), may hold values from 0 to 63, all different within a row; in each aligned block of 128 rows (0 to 127, 128 to 255, ..., all dimensions but the last counted through in order) at most 5 rows name the same one
- hidden_grad: bfloat16 [4, 8192, 2, 1024], P('dp', 'expert'), may hold values from -1.5 to 1.5
- w_gate: bfloat16 [64, 3584, 1024], P('expert', None, 'dp'), may hold values from -0.09375 to 0.09375
- w_up: bfloat16 [64, 3584, 1024], P('expert', None, 'dp'), may hold values from -0.09375 to 0.09375
Outputs:
- token_grad: bfloat16 [4, 8192, 3584], P('dp', 'expert')
- gate_grad: bfloat16 [64, 3584, 1024], P('expert', None, 'dp')
- up_grad: bfloat16 [64, 3584, 1024], P('expert', None, 'dp')
The draws below stay inside these ranges and needn't reach their ends.
Inputs may be any that keep to these rules, and one draw needn't show every extreme that they name: `routes`: each row names 2 different experts. In each aligned block of 128 rows (the rows of one device) no expert is named by more than 5 rows, a bound that some block reaches.
All inputs are finite; a program needn't handle non-finite values.
Results may differ from the reference program's by a relative error of at most 0.0059.
Values may be sent and summed in bfloat16 or wider, within the bound.
No kernel may reach another device: no remote copies, remote signals or barrier semaphores. Data moves between devices by JAX's collectives and lax.ppermute only.
A program may use at most 128 MiB of HBM per device.

```python
import math
import jax
import jax.numpy as jnp
import numpy as np
from jax import lax

D = 3584
F = 1024
TOP = 2
TOK_DEV = 128
EXPERTS = 64
GTOK = 8192
MOST = 5
SLOTS = 320
N_EXPERT = 64
N_DP = 4


def block_levels(own_key, shape, cuts, low, high):
    level = 1.0
    for dim, blocks in cuts:
        heights = jax.random.uniform(jax.random.fold_in(jax.random.fold_in(own_key, 6), dim), (blocks,), jnp.float32, low / len(cuts), high / len(cuts))
        level = level * jnp.repeat(jnp.exp(heights), shape[dim] // blocks).reshape((-1,) + (1,) * (len(shape) - 1 - dim))
    return level


def deal_out(rng, own, number, rows, amount, top, bound, slope):
    order = jax.random.permutation(rng, amount)
    crowded, common = load_shares(amount, rows * top, bound, slope, True), load_shares(amount, rows * top, bound, slope, False)
    places = jnp.arange(amount)

    def named(sizes, rotation):
        used = int((sizes > 0).sum())
        fixed = max(1, used // 4)
        passed = fixed + (places - fixed + rotation * (used - fixed)) % max(1, amount - fixed)
        return jnp.zeros((amount,), jnp.int32).at[order[jnp.where(places < fixed, places, passed)]].set(jnp.asarray(sizes, jnp.int32))

    sizes = jnp.where(number % 4 == 0, named(crowded, number // 4), named(common, number - number // 4 - 1))
    mixed = jax.random.permutation(jax.random.fold_in(own, 3), amount)
    donor, taker = mixed[0:amount // 2 * 2:2], mixed[1:amount // 2 * 2:2]
    slack = jnp.minimum(sizes[donor] - 1, bound - sizes[taker]) // 2
    slack = jnp.where((donor == order[0]) | (taker == order[0]) | (sizes[taker] == 0), 0, jnp.maximum(slack, 0))
    passed = jax.random.randint(jax.random.fold_in(own, 4), (amount // 2,), 0, 1 << 20) % (slack + 1)
    sizes = sizes.at[donor].add(-passed).at[taker].add(passed)
    items = jnp.searchsorted(jnp.cumsum(sizes), jnp.arange(rows * top), side="right").astype(jnp.int32)
    listing = items.reshape(top, rows).T
    listing = listing[jax.random.permutation(jax.random.fold_in(own, 1), rows)]
    rotation = jax.random.randint(jax.random.fold_in(own, 2), (rows, 1), 0, top)
    return jnp.take_along_axis(listing, (jnp.arange(top)[None, :] + rotation) % top, axis=1)


def load_shares(number_of, total, reach, skew, full):
    weights = [(1 << 20) // math.isqrt(grade ** skew) + 1 for grade in range(1, number_of + 1)]
    largest = reach if full else min(reach, max(-(-total // number_of), total * weights[0] // sum(weights)))
    least = 1 if total - largest >= number_of - 1 else 0
    counts, spare = [largest] + [least] * (number_of - 1), total - largest - least * (number_of - 1)
    while spare > 0:
        candidates = [i for i in range(1, number_of) if counts[i] < largest] or [i for i in range(1, number_of) if counts[i] < reach]
        pool, left = sum([weights[i] for i in candidates]), spare
        for i in candidates:
            more = min(reach - counts[i], max(1, left * weights[i] // pool), spare)
            counts[i] = counts[i] + more
            spare = spare - more
    return np.array(counts)


def gaussian(stream_key, extent, deviation, reach, split=(), held_as=jnp.bfloat16):
    result = deviation * jax.random.normal(stream_key, extent, jnp.float32)
    if split:
        result = result * block_levels(stream_key, extent, split, -0.22, 0.18)
    return jnp.clip(result, -reach, reach).astype(held_as)


def setup_inputs(seed: int = 0) -> dict:
    arg_keys = jax.random.split(jax.random.key(seed), 6)
    tokens = gaussian(arg_keys[0], (N_DP, GTOK, D), 1.0, 6.0, ((0, 4), (1, 64)))
    routes_keys = jax.random.split(jax.random.fold_in(arg_keys[1], 1), N_DP * GTOK // TOK_DEV)
    routes_turns = jax.random.permutation(jax.random.fold_in(arg_keys[1], 3), N_DP * GTOK // TOK_DEV)
    routes = jax.vmap(lambda own, number: deal_out(jax.random.fold_in(arg_keys[1], 2), own, number, TOK_DEV, N_EXPERT, TOP, MOST, 2))(routes_keys, routes_turns).reshape((N_DP, GTOK, TOP))
    hidden_grad = gaussian(arg_keys[2], (N_DP, GTOK, TOP, F), 0.25, 1.5, ((0, 4), (1, 64)))
    w_gate = gaussian(arg_keys[3], (EXPERTS, D, F), D ** -0.5, 0.09375, ((0, 64), (2, 4)))
    w_up = gaussian(arg_keys[4], (EXPERTS, D, F), D ** -0.5, 0.09375, ((0, 64), (2, 4)))
    return {"tokens": tokens, "routes": routes, "hidden_grad": hidden_grad, "w_gate": w_gate, "w_up": w_up}


def route_slots(expert_ids):
    flat_ids = expert_ids.reshape(N_EXPERT, TOK_DEV * TOP)
    onehot = (flat_ids[:, :, None] == jnp.arange(N_EXPERT, dtype=jnp.int32)[None, None, :]).astype(jnp.int32)
    ranking = jnp.sum(jnp.cumsum(onehot, axis=1) * onehot, axis=2) - 1
    slot_pos = jnp.arange(N_EXPERT, dtype=jnp.int32)[:, None] * MOST + ranking
    return flat_ids.reshape(-1).astype(jnp.int32), slot_pos.reshape(-1).astype(jnp.int32)


def local_grads(inputs, cotangent, weight_g, weight_u):
    gate_pre = jnp.dot(inputs, weight_g, preferred_element_type=jnp.float32)
    up_pre = jnp.dot(inputs, weight_u, preferred_element_type=jnp.float32)
    sigmoid_g = jax.nn.sigmoid(gate_pre)
    upstream = cotangent.astype(jnp.float32)
    up_cot = (upstream * gate_pre * sigmoid_g).astype(jnp.bfloat16)
    gate_cot = (upstream * up_pre * sigmoid_g * (1.0 + gate_pre * (1.0 - sigmoid_g))).astype(jnp.bfloat16)
    return gate_cot, up_cot


def round_partial(term):
    narrow = lax.optimization_barrier(term.astype(jnp.bfloat16))
    return narrow.astype(jnp.float32)


def reference(tokens, routes, hidden_grad, w_gate, w_up):
    total = GTOK * TOP
    tables = []
    expert_lists = []
    slot_lists = []
    for group_index in range(N_DP):
        expert_ids, slot_pos = route_slots(routes[group_index])
        table = jnp.full((N_EXPERT, SLOTS), total, dtype=jnp.int32)
        table = table.at[expert_ids, slot_pos].set(jnp.arange(total, dtype=jnp.int32))
        tables.append(table)
        expert_lists.append(expert_ids)
        slot_lists.append(slot_pos)
    table_all = jnp.stack(tables, axis=1)
    inputs_pad = jnp.concatenate([tokens, jnp.zeros((N_DP, 1, D), jnp.bfloat16)], axis=1)
    cot_pad = jnp.concatenate([hidden_grad.reshape(N_DP, total, F), jnp.zeros((N_DP, 1, F), jnp.bfloat16)], axis=1)

    def per_expert(operands):
        weight_g, weight_u, table = operands
        acc_gate = jnp.zeros((D, F), jnp.float32)
        acc_up = jnp.zeros((D, F), jnp.float32)
        results = []
        for group_index in range(N_DP):
            entry = table[group_index]
            chosen = inputs_pad[group_index][entry // TOP]
            cotangent = cot_pad[group_index][entry]
            gate_cot, up_cot = local_grads(chosen, cotangent, weight_g, weight_u)
            routed = jnp.dot(gate_cot, weight_g.T, preferred_element_type=jnp.float32)
            routed = routed + jnp.dot(up_cot, weight_u.T, preferred_element_type=jnp.float32)
            results.append(routed.astype(jnp.bfloat16))
            acc_gate = acc_gate + round_partial(jnp.dot(chosen.T, gate_cot, preferred_element_type=jnp.float32))
            acc_up = acc_up + round_partial(jnp.dot(chosen.T, up_cot, preferred_element_type=jnp.float32))
        return jnp.stack(results), acc_gate.astype(jnp.bfloat16), acc_up.astype(jnp.bfloat16)

    routed_all, gate_grad, up_grad = lax.map(per_expert, (w_gate, w_up, table_all))
    grads = []
    for group_index in range(N_DP):
        picked = routed_all[expert_lists[group_index], group_index, slot_lists[group_index]]
        picked = picked.astype(jnp.float32).reshape(GTOK, TOP, D)
        grads.append(jnp.sum(picked, axis=1).astype(jnp.bfloat16))
    token_grad = jnp.stack(grads)
    return token_grad, gate_grad, up_grad
```

```python
import jax
import jax.numpy as jnp
from jax import lax
from jax.sharding import Mesh, PartitionSpec as P

RING = ("zl", "dp")
PLANE = ("x", "y", "core")
EXPERT = ("x", "zl", "y", "core")
CAP = 5


def shift(value, step):
    n, far = lax.axis_size(RING), lax.axis_size("dp")
    at = [(z % 2) * far + z // 2 for z in range(n)]
    return lax.ppermute(value, RING, [(at[z], at[(z + step) % n]) for z in range(n)])


def half_of(width):
    return (width // 128 + 1) // 2 * 128


def ring_gather(value):
    n = lax.axis_size(RING)
    got = {0: value}
    fore = back = value
    for step in range(1, n // 2):
        fore = shift(fore, 1)
        back = shift(back, -1)
        got[n - step] = fore
        got[step] = back
    half = half_of(value.shape[1])
    left = shift(fore[:, :half], 1)
    right = shift(back[:, half:], -1)
    got[n // 2] = jnp.concatenate([left, right], axis=1)
    return [got[i] for i in range(n)]


def ring_scatter(parts):
    n = lax.axis_size(RING)
    mid = n // 2
    half = half_of(parts[0].shape[1])
    bf = jnp.bfloat16
    fore = shift(parts[mid][:, :half].astype(bf), 1).astype(jnp.float32)
    back = shift(parts[mid][:, half:].astype(bf), -1).astype(jnp.float32)
    fore = jnp.concatenate([parts[mid - 1][:, :half] + fore, parts[mid - 1][:, half:]], axis=1)
    back = jnp.concatenate([parts[mid + 1][:, :half], parts[mid + 1][:, half:] + back], axis=1)
    for step in range(mid - 1, 0, -1):
        fore = shift(fore.astype(bf), 1).astype(jnp.float32) + parts[step - 1]
        back = shift(back.astype(bf), -1).astype(jnp.float32)
        if step > 1:
            back = back + parts[n - step + 1]
    return (fore + back).astype(bf)


def exchange(rows):
    n = lax.axis_size(PLANE)
    out = lax.all_to_all(rows.reshape(n, -1, rows.shape[1]), PLANE, 0, 0, tiled=True)
    return out.reshape(rows.shape)


def slot_matrices(ids, own):
    blocks = lax.axis_size(RING)
    tokens = ids.shape[0]
    rows = tokens // blocks
    n = own.shape[0]
    named = [(ids[:, k][None, :] == own[:, None]) for k in range(2)]
    member = (named[0] | named[1]).astype(jnp.bfloat16).reshape(n * blocks, rows)
    before = (jnp.arange(rows)[:, None] < jnp.arange(rows)[None, :]).astype(jnp.bfloat16)
    rank = jnp.dot(member, before, preferred_element_type=jnp.float32).reshape(n, 1, tokens)
    slot = jnp.arange(CAP * blocks)[:, None]
    block = (jnp.arange(tokens) // rows)[None, :]
    wanted = jnp.where(slot % blocks == block, slot // blocks, -1).astype(jnp.float32)
    hit = rank == wanted[None]
    return [
        (hit & named[k][:, None, :]).astype(jnp.bfloat16).reshape(n * CAP * blocks, tokens)
        for k in range(2)
    ]


def on_device(tokens, routes, hidden_grad, w_gate, w_up):
    bf, f32 = jnp.bfloat16, jnp.float32
    blocks = lax.axis_size(RING)
    n = lax.axis_size(PLANE)
    x = tokens[0]
    tok, width = x.shape
    cut = width // 2
    wg, wu = w_gate[0], w_up[0]
    share = wg.shape[1]

    ids = jnp.pad(routes[0].astype(bf), ((0, 0), (0, 126)))
    first = ring_gather(jnp.concatenate([x[:, :cut], ids], axis=1))
    x2 = x[:, cut:]
    x2, first = lax.optimization_barrier((x2, first))
    second = ring_gather(x2)

    cot = hidden_grad[0].reshape(tok, 2, -1, share).transpose(2, 0, 1, 3).reshape(-1, tok, 2 * share)
    cot = lax.all_to_all(jnp.concatenate([cot, cot], axis=0), RING, 0, 0, tiled=True)
    cot = cot.reshape(2, -1, tok, 2 * share).transpose(1, 0, 2, 3).reshape(blocks, tok, 2 * share)
    place = lax.axis_index("dp") * 2 + lax.axis_index("zl")
    cot = lax.dynamic_slice_in_dim(jnp.concatenate([cot, cot], axis=0), place, blocks, axis=0)
    cot = cot.reshape(blocks * tok, 2 * share)

    first = jnp.concatenate(first, axis=0)
    second = jnp.concatenate(second, axis=0)
    le = jnp.arange(n)
    own = (le // 8) * 16 + lax.axis_index("zl") * 8 + le % 8
    pick0, pick1 = slot_matrices(first[:, cut : cut + 2].astype(jnp.int32), own)
    pick = pick0 + pick1

    send1 = jnp.dot(pick, first[:, :cut], preferred_element_type=f32).astype(bf)
    recv1 = exchange(send1)
    send2 = jnp.dot(pick, second, preferred_element_type=f32).astype(bf)
    sendc = (
        jnp.dot(pick0, cot[:, :share], preferred_element_type=f32)
        + jnp.dot(pick1, cot[:, share:], preferred_element_type=f32)
    ).astype(bf)
    recv2 = exchange(jnp.concatenate([send2, sendc], axis=1))
    rows2 = recv2[:, : width - cut]
    upstream = recv2[:, width - cut :].astype(f32)

    gate_pre = jnp.dot(recv1, wg[:cut], preferred_element_type=f32) + jnp.dot(
        rows2, wg[cut:], preferred_element_type=f32
    )
    up_pre = jnp.dot(recv1, wu[:cut], preferred_element_type=f32) + jnp.dot(
        rows2, wu[cut:], preferred_element_type=f32
    )
    sig = jax.nn.sigmoid(gate_pre)
    up_cot = (upstream * gate_pre * sig).astype(bf)
    gate_cot = (upstream * up_pre * sig * (1.0 + gate_pre * (1.0 - sig))).astype(bf)

    def back(lo, hi):
        routed = jnp.dot(gate_cot, wg[lo:hi].T, preferred_element_type=f32) + jnp.dot(
            up_cot, wu[lo:hi].T, preferred_element_type=f32
        )
        return exchange(routed.astype(bf))

    def home(returned):
        summed = lax.dot_general(
            pick, returned, (((0,), (0,)), ((), ())), preferred_element_type=f32
        )
        return ring_scatter([summed[i * tok : (i + 1) * tok] for i in range(blocks)])

    ret1 = back(0, cut)
    ret2 = back(cut, width)
    grad1 = home(ret1)
    grad2 = home(ret2)
    token_grad = jnp.concatenate([grad1, grad2], axis=1)

    def weight_grad(c):
        lo = lax.dot_general(recv1, c, (((0,), (0,)), ((), ())), preferred_element_type=f32)
        hi = lax.dot_general(rows2, c, (((0,), (0,)), ((), ())), preferred_element_type=f32)
        return jnp.concatenate([lo.astype(bf), hi.astype(bf)], axis=0)

    return token_grad[None], weight_grad(gate_cot)[None], weight_grad(up_cot)[None]


def solution(mesh):
    fine = Mesh(mesh.devices.reshape(4, 2, 4, 2, 4), ("x", "zl", "y", "core", "dp"))
    return jax.shard_map(
        on_device,
        mesh=fine,
        in_specs=(
            P("dp", EXPERT, None),
            P("dp", EXPERT, None),
            P("dp", EXPERT, None, None),
            P(EXPERT, None, "dp"),
            P(EXPERT, None, "dp"),
        ),
        out_specs=(P("dp", EXPERT, None), P(EXPERT, None, "dp"), P(EXPERT, None, "dp")),
        check_vma=False,
    )
```

```python
import jax
import jax.numpy as jnp
from jax import lax
from jax.sharding import Mesh, PartitionSpec as P

RING = ("zl", "dp")
PLANE = ("x", "y", "core")
EXPERT = ("x", "zl", "y", "core")
CAP = 5
CUT = 18


def shift(value, step):
    n, far = lax.axis_size(RING), lax.axis_size("dp")
    at = [(z % 2) * far + z // 2 for z in range(n)]
    return lax.ppermute(value, RING, [(at[z], at[(z + step) % n]) for z in range(n)])


def half_of(width):
    return (width // 128 + 1) // 2 * 128


def ring_gather(value):
    n = lax.axis_size(RING)
    got = {0: value}
    fore = back = value
    for step in range(1, n // 2):
        fore = shift(fore, 1)
        back = shift(back, -1)
        got[n - step] = fore
        got[step] = back
    half = half_of(value.shape[1])
    left = shift(fore[:, :half], 1)
    right = shift(back[:, half:], -1)
    got[n // 2] = jnp.concatenate([left, right], axis=1)
    return [got[i] for i in range(n)]


def ring_scatter(parts):
    n = lax.axis_size(RING)
    mid = n // 2
    half = half_of(parts[0].shape[1])
    bf = jnp.bfloat16
    fore = shift(parts[mid][:, :half].astype(bf), 1).astype(jnp.float32)
    back = shift(parts[mid][:, half:].astype(bf), -1).astype(jnp.float32)
    fore = jnp.concatenate([parts[mid - 1][:, :half] + fore, parts[mid - 1][:, half:]], axis=1)
    back = jnp.concatenate([parts[mid + 1][:, :half], parts[mid + 1][:, half:] + back], axis=1)
    for step in range(mid - 1, 0, -1):
        fore = shift(fore.astype(bf), 1).astype(jnp.float32) + parts[step - 1]
        back = shift(back.astype(bf), -1).astype(jnp.float32)
        if step > 1:
            back = back + parts[n - step + 1]
    return (fore + back).astype(bf)


def row_gather(same, other):
    rows, half = same.shape[0], half_of(same.shape[1])
    both = jnp.concatenate([same, other], axis=0)
    fore1, back1 = shift(both, 1), shift(both, -1)
    fore2, back2 = shift(fore1, 1), shift(back1, -1)
    fore3, back3 = shift(fore2[rows:], 1), shift(back2[rows:], -1)
    left, right = shift(fore2[:rows, :half], 1), shift(back2[:rows, half:], -1)
    left, right = shift(left, 1), shift(right, -1)
    far = jnp.concatenate([left, right], axis=1)
    return [same, back1[rows:], back2[:rows], back3, far, fore3, fore2[:rows], fore1[rows:]]


def row_scatter(parts):
    bf, f32 = jnp.bfloat16, jnp.float32
    rows, half = parts[0].shape[0], half_of(parts[0].shape[1])
    left, right = shift(parts[4][:, :half], 1), shift(parts[4][:, half:], -1)
    fore, back = shift(parts[3], 1), shift(parts[5], -1)
    left, right = shift(left, 1), shift(right, -1)
    two, six = parts[2].astype(f32), parts[6].astype(f32)
    sum2 = jnp.concatenate([two[:, :half] + left.astype(f32), two[:, half:]], axis=1).astype(bf)
    sum6 = jnp.concatenate([six[:, :half], six[:, half:] + right.astype(f32)], axis=1).astype(bf)
    fore = shift(jnp.concatenate([sum2, fore], axis=0), 1)
    back = shift(jnp.concatenate([sum6, back], axis=0), -1)
    one = (fore[rows:].astype(f32) + parts[1].astype(f32)).astype(bf)
    seven = (back[rows:].astype(f32) + parts[7].astype(f32)).astype(bf)
    fore = shift(jnp.concatenate([fore[:rows], one], axis=0), 1).astype(f32)
    back = shift(jnp.concatenate([back[:rows], seven], axis=0), -1).astype(f32)
    total = fore + back
    same = total[:rows] + parts[0].astype(f32)
    return same.astype(bf), total[rows:].astype(bf)


def exchange(rows):
    n = lax.axis_size(PLANE)
    out = lax.all_to_all(rows.reshape(n, -1, rows.shape[1]), PLANE, 0, 0, tiled=True)
    return out.reshape(rows.shape)


def ranks(ids, own, rows):
    named = [ids[k][None, :] == own[:, None] for k in range(2)]
    member = (named[0] | named[1]).astype(jnp.bfloat16)
    before = (jnp.arange(rows)[:, None] < jnp.arange(rows)[None, :]).astype(jnp.bfloat16)
    rank = jnp.dot(member.reshape(-1, rows), before, preferred_element_type=jnp.float32)
    return named, rank.reshape(member.shape)


def plane_slots(ids, own, blocks):
    rows = ids.shape[1] // blocks
    named, rank = ranks(ids, own, rows)
    slot = jnp.arange(CAP * blocks)[:, None]
    block = (jnp.arange(ids.shape[1]) // rows)[None, :]
    wanted = jnp.where(slot % blocks == block, slot // blocks, -1).astype(jnp.float32)
    hit = (rank[:, None, :] == wanted[None]) & (named[0] | named[1])[:, None, :]
    return hit.astype(jnp.bfloat16).reshape(-1, ids.shape[1])


def own_slots(ids, own):
    named, rank = ranks(ids, own, ids.shape[1])
    hit = rank[:, None, :] == jnp.arange(8, dtype=jnp.float32)[None, :, None]
    return [
        (hit & named[k][:, None, :]).astype(jnp.bfloat16).reshape(-1, ids.shape[1])
        for k in range(2)
    ]


def dot(a, b):
    return jnp.dot(a, b, preferred_element_type=jnp.float32)


def dot_t(a, b):
    return lax.dot_general(a, b, (((0,), (0,)), ((), ())), preferred_element_type=jnp.float32)


def on_device(tokens, routes, hidden_grad, w_gate, w_up):
    bf, f32 = jnp.bfloat16, jnp.float32
    blocks, n = lax.axis_size(RING), lax.axis_size(PLANE)
    zl, zh = lax.axis_index("zl"), lax.axis_index("dp")
    x = tokens[0]
    tok, width = x.shape
    cut = width * CUT // 28
    rest = width - cut
    wg, wu = w_gate[0], w_up[0]
    share = wg.shape[1]
    le = jnp.arange(n)
    plane = (le // 8) * 16 + le % 8
    pair = jnp.stack([zl, 1 - zl])

    ids = routes[0].T
    ring = ring_gather(x[:, :cut])
    all_ids = [ids] + [shift(ids, -i) for i in range(1, blocks)]
    pick = plane_slots(jnp.concatenate(all_ids, axis=1), plane + zl * 8, blocks)

    own0, own1 = own_slots(ids, (plane[:, None] + 8 * pair[None, :]).reshape(-1))
    own = own0 + own1
    grads = hidden_grad[0]
    near = jnp.concatenate(
        [dot(own, x[:, cut:]).astype(bf), (dot(own0, grads[:, 0]) + dot(own1, grads[:, 1])).astype(bf)],
        axis=1,
    )
    near = exchange(near).reshape(n, 2, 8, -1)[:, :, :CAP]
    near = near.transpose(1, 0, 2, 3).reshape(2, n * CAP, -1)

    near, ring = lax.optimization_barrier((near, ring))
    rows_b = row_gather(near[0, :, :rest], near[1, :, :rest])
    rows_b = jnp.stack(rows_b, axis=1).reshape(-1, rest)
    ups = []
    for i in range(blocks):
        to = (zh * 2 + zl + blocks - i) % blocks // 2
        part = lax.dynamic_slice_in_dim(near[i % 2, :, rest:], to * share, share, axis=1)
        ups.append(part if i == 0 else shift(part, -i))
    upstream = jnp.stack(ups, axis=1).reshape(-1, share).astype(f32)

    rows_a = exchange(dot(pick, jnp.concatenate(ring, axis=0)).astype(bf))

    gate_pre = dot(rows_a, wg[:cut]) + dot(rows_b, wg[cut:])
    up_pre = dot(rows_a, wu[:cut]) + dot(rows_b, wu[cut:])
    sig = jax.nn.sigmoid(gate_pre)
    up_cot = (upstream * gate_pre * sig).astype(bf)
    gate_cot = (upstream * up_pre * sig * (1.0 + gate_pre * (1.0 - sig))).astype(bf)

    def routed(g, u, lo, hi):
        return (dot(g, wg[lo:hi].T) + dot(u, wu[lo:hi].T)).astype(bf)

    back_b = routed(gate_cot, up_cot, cut, width)
    gate_cot, up_cot, back_b = lax.optimization_barrier((gate_cot, up_cot, back_b))
    back_a = exchange(routed(gate_cot, up_cot, 0, cut))
    back_b = back_b.reshape(n * CAP, blocks, rest)
    same, other = row_scatter([back_b[:, i] for i in range(blocks)])
    back_a, same, other = lax.optimization_barrier((back_a, same, other))

    back_b = jnp.stack([same.reshape(n, CAP, rest), other.reshape(n, CAP, rest)], axis=1)
    back_b = exchange(jnp.pad(back_b, ((0, 0), (0, 0), (0, 8 - CAP), (0, 0))).reshape(-1, rest))
    summed = dot_t(pick, back_a)
    grad_a = ring_scatter([summed[i * tok : (i + 1) * tok] for i in range(blocks)])
    grad_b = dot_t(own, back_b).astype(bf)
    token_grad = jnp.concatenate([grad_a, grad_b], axis=1)

    def weight_grad(c):
        return jnp.concatenate([dot_t(rows_a, c).astype(bf), dot_t(rows_b, c).astype(bf)], axis=0)

    return token_grad[None], weight_grad(gate_cot)[None], weight_grad(up_cot)[None]


def solution(mesh):
    fine = Mesh(mesh.devices.reshape(4, 2, 4, 2, 4), ("x", "zl", "y", "core", "dp"))
    return jax.shard_map(
        on_device,
        mesh=fine,
        in_specs=(
            P("dp", EXPERT, None),
            P("dp", EXPERT, None),
            P("dp", EXPERT, None, None),
            P(EXPERT, None, "dp"),
            P(EXPERT, None, "dp"),
        ),
        out_specs=(P("dp", EXPERT, None), P(EXPERT, None, "dp"), P(EXPERT, None, "dp")),
        check_vma=False,
    )
```

```python
import jax
import jax.numpy as jnp
from jax import lax
from jax.experimental import pallas as pl
from jax.experimental.pallas import tpu as pltpu
from jax.sharding import Mesh, PartitionSpec as P

RING = ("zl", "dp")
PLANE = ("x", "y", "core")
EXPERT = ("x", "zl", "y", "core")
CAP = 5
CUT = 20
CUT_BACK = 18


def shift(value, step):
    n, far = lax.axis_size(RING), lax.axis_size("dp")
    at = [(z % 2) * far + z // 2 for z in range(n)]
    return lax.ppermute(value, RING, [(at[z], at[(z + step) % n]) for z in range(n)])


def half_of(width):
    return (width // 128 + 1) // 2 * 128


def ring_gather(value):
    n = lax.axis_size(RING)
    got = {0: value}
    fore = back = value
    for step in range(1, n // 2):
        fore = shift(fore, 1)
        back = shift(back, -1)
        got[n - step] = fore
        got[step] = back
    half = half_of(value.shape[1])
    left = shift(fore[:, :half], 1)
    right = shift(back[:, half:], -1)
    got[n // 2] = jnp.concatenate([left, right], axis=1)
    return [got[i] for i in range(n)]


def ring_scatter(parts):
    n = lax.axis_size(RING)
    mid = n // 2
    half = half_of(parts[0].shape[1])
    bf = jnp.bfloat16
    fore = shift(parts[mid][:, :half].astype(bf), 1).astype(jnp.float32)
    back = shift(parts[mid][:, half:].astype(bf), -1).astype(jnp.float32)
    fore = jnp.concatenate([parts[mid - 1][:, :half] + fore, parts[mid - 1][:, half:]], axis=1)
    back = jnp.concatenate([parts[mid + 1][:, :half], parts[mid + 1][:, half:] + back], axis=1)
    for step in range(mid - 1, 0, -1):
        fore = shift(fore.astype(bf), 1).astype(jnp.float32) + parts[step - 1]
        back = shift(back.astype(bf), -1).astype(jnp.float32)
        if step > 1:
            back = back + parts[n - step + 1]
    return (fore + back).astype(bf)


def exchange(rows):
    n = lax.axis_size(PLANE)
    out = lax.all_to_all(rows.reshape(n, -1, rows.shape[1]), PLANE, 0, 0, tiled=True)
    return out.reshape(rows.shape)


def ranks(ids, own, rows):
    named = [ids[k][None, :] == own[:, None] for k in range(2)]
    member = (named[0] | named[1]).astype(jnp.bfloat16)
    before = (jnp.arange(rows)[:, None] < jnp.arange(rows)[None, :]).astype(jnp.bfloat16)
    rank = jnp.dot(member.reshape(-1, rows), before, preferred_element_type=jnp.float32)
    return named, rank.reshape(member.shape)


def plane_slots(ids, own, blocks):
    rows = ids.shape[1] // blocks
    named, rank = ranks(ids, own, rows)
    slot = jnp.arange(CAP * blocks)[:, None]
    block = (jnp.arange(ids.shape[1]) // rows)[None, :]
    wanted = jnp.where(slot % blocks == block, slot // blocks, -1).astype(jnp.float32)
    hit = (rank[:, None, :] == wanted[None]) & (named[0] | named[1])[:, None, :]
    return hit.astype(jnp.bfloat16).reshape(-1, ids.shape[1])


def own_slots(ids, own):
    named, rank = ranks(ids, own, ids.shape[1])
    hit = rank[:, None, :] == jnp.arange(8, dtype=jnp.float32)[None, :, None]
    return [
        (hit & named[k][:, None, :]).astype(jnp.bfloat16).reshape(-1, ids.shape[1])
        for k in range(2)
    ]


def dot(a, b):
    return jnp.dot(a, b, preferred_element_type=jnp.float32)


def dot_nt(a, b):
    return lax.dot_general(a, b, (((1,), (1,)), ((), ())), preferred_element_type=jnp.float32)


def dot_t(a, b):
    return lax.dot_general(a, b, (((0,), (0,)), ((), ())), preferred_element_type=jnp.float32)


def grads_kernel(a_ref, b_ref, wg_ref, wu_ref, gate_ref, up_ref, back_ref):
    bf, f32 = jnp.bfloat16, jnp.float32
    cut = a_ref.shape[1]
    rest = wg_ref.shape[0] - cut
    gate_pre = dot(a_ref[...], wg_ref[:cut]) + dot(b_ref[:, :rest], wg_ref[cut:])
    up_pre = dot(a_ref[...], wu_ref[:cut]) + dot(b_ref[:, :rest], wu_ref[cut:])
    upstream = b_ref[:, rest:].astype(f32)
    sig = 1.0 / (1.0 + jnp.exp(-gate_pre))
    up_cot = (upstream * gate_pre * sig).astype(bf)
    gate_cot = (upstream * up_pre * sig * (1.0 + gate_pre * (1.0 - sig))).astype(bf)
    up_ref[...] = up_cot
    gate_ref[...] = gate_cot
    part = 256
    for lo in range(0, back_ref.shape[1], part):
        back_ref[:, lo : lo + part] = (
            dot_nt(gate_cot, wg_ref[lo : lo + part]) + dot_nt(up_cot, wu_ref[lo : lo + part])
        ).astype(bf)


def local_grads(rows_a, rows_b, wg, wu, back):
    bf = jnp.bfloat16
    rows = rows_a.shape[0]
    width, share = wg.shape
    step = 256
    row = lambda n: pl.BlockSpec((step, n), lambda i: (i, 0))
    whole = pl.BlockSpec((width, share), lambda i: (0, 0))
    return pl.pallas_call(
        grads_kernel,
        grid=(rows // step,),
        in_specs=[row(rows_a.shape[1]), row(rows_b.shape[1]), whole, whole],
        out_specs=[row(share), row(share), row(back)],
        out_shape=[
            jax.ShapeDtypeStruct((rows, share), bf),
            jax.ShapeDtypeStruct((rows, share), bf),
            jax.ShapeDtypeStruct((rows, back), bf),
        ],
        compiler_params=pltpu.CompilerParams(vmem_limit_bytes=32 * 2**20),
        cost_estimate=pl.CostEstimate(
            flops=4 * rows * share * (width + back), bytes_accessed=2 * rows * 2 * width, transcendentals=rows * share
        ),
    )(rows_a, rows_b, wg, wu)


def on_device(tokens, routes, hidden_grad, w_gate, w_up):
    bf, f32 = jnp.bfloat16, jnp.float32
    blocks, n = lax.axis_size(RING), lax.axis_size(PLANE)
    zl, zh = lax.axis_index("zl"), lax.axis_index("dp")
    x = tokens[0]
    tok, width = x.shape
    cut = width * CUT // 28
    rest = width - cut
    wg, wu = w_gate[0], w_up[0]
    share = wg.shape[1]
    le = jnp.arange(n)
    plane = (le // 8) * 16 + le % 8
    pair = jnp.stack([zl, 1 - zl])

    ids = routes[0].T
    all_ids = lax.all_gather(ids, RING)
    ring = ring_gather(x[:, :cut])

    own0, own1 = own_slots(ids, (plane[:, None] + 8 * pair[None, :]).reshape(-1))
    own = own0 + own1
    grads = hidden_grad[0]
    near = jnp.concatenate(
        [dot(own, x[:, cut:]).astype(bf), (dot(own0, grads[:, 0]) + dot(own1, grads[:, 1])).astype(bf)],
        axis=1,
    )
    near = exchange(near).reshape(n, 2, 8, -1)[:, :, :CAP]
    near = near.transpose(1, 0, 2, 3).reshape(2, n * CAP, -1)

    all_ids = all_ids.reshape(2, -1, 2, tok).transpose(2, 1, 0, 3).reshape(2, -1)
    all_ids = jnp.concatenate([all_ids, all_ids], axis=1)
    all_ids = lax.dynamic_slice_in_dim(all_ids, (zh * 2 + zl) * tok, blocks * tok, axis=1)
    pick = plane_slots(all_ids, plane + zl * 8, blocks)

    near, ring = lax.optimization_barrier((near, ring))
    rows_a = exchange(dot(pick, jnp.concatenate(ring, axis=0)).astype(bf))

    got = []
    for i in range(blocks):
        to = (zh * 2 + zl + blocks - i) % blocks // 2
        part = lax.dynamic_slice_in_dim(near[i % 2, :, rest:], to * share, share, axis=1)
        part = jnp.concatenate([near[i % 2, :, :rest], part], axis=1)
        got.append(part if i == 0 else shift(part, -i))
    got = jnp.stack(got, axis=1).reshape(n * CAP * blocks, -1)
    rows_b = got[:, :rest]

    cut = width * CUT_BACK // 28
    rest = width - cut
    gate_cot, up_cot, back_a = local_grads(rows_a, got, wg, wu, cut)
    back_a = exchange(back_a)

    def by_block(c):
        return c.reshape(n * CAP, blocks, share).transpose(1, 0, 2).reshape(-1, share)

    back_b = (dot_nt(by_block(gate_cot), wg[cut:]) + dot_nt(by_block(up_cot), wu[cut:])).astype(bf)
    back_b = back_b.reshape(blocks, n * CAP, rest)
    home = [back_b[i] if i == 0 else shift(back_b[i], i) for i in range(blocks)]
    home = [h.astype(f32) for h in home]
    same = (home[0] + home[2] + home[4] + home[6]).astype(bf)
    other = (home[1] + home[3] + home[5] + home[7]).astype(bf)
    back_a, same, other = lax.optimization_barrier((back_a, same, other))

    back_b = jnp.stack([same.reshape(n, CAP, rest), other.reshape(n, CAP, rest)], axis=1)
    back_b = exchange(jnp.pad(back_b, ((0, 0), (0, 0), (0, 8 - CAP), (0, 0))).reshape(-1, rest))
    summed = dot_t(pick, back_a)
    grad_a = ring_scatter([summed[i * tok : (i + 1) * tok] for i in range(blocks)])
    grad_b = dot_t(own, back_b).astype(bf)
    token_grad = jnp.concatenate([grad_a, grad_b], axis=1)

    def weight_grad(c):
        return jnp.concatenate([dot_t(rows_a, c).astype(bf), dot_t(rows_b, c).astype(bf)], axis=0)

    return token_grad[None], weight_grad(gate_cot)[None], weight_grad(up_cot)[None]


def solution(mesh):
    fine = Mesh(mesh.devices.reshape(4, 2, 4, 2, 4), ("x", "zl", "y", "core", "dp"))
    return jax.shard_map(
        on_device,
        mesh=fine,
        in_specs=(
            P("dp", EXPERT, None),
            P("dp", EXPERT, None),
            P("dp", EXPERT, None, None),
            P(EXPERT, None, "dp"),
            P(EXPERT, None, "dp"),
        ),
        out_specs=(P("dp", EXPERT, None), P(EXPERT, None, "dp"), P(EXPERT, None, "dp")),
        check_vma=False,
    )
```

```python
import functools

import jax
import jax.numpy as jnp
from jax import lax
from jax.experimental import pallas as pl
from jax.experimental.pallas import tpu as pltpu
from jax.sharding import Mesh, PartitionSpec as P

RING = ("zl", "dp")
PLANE = ("x", "y", "core")
EXPERT = ("x", "zl", "y", "core")
CAP = 5
VMEM = 56 * 2**20
CUT = 18
CUT_BACK = 17


def shift(value, step):
    n, far = lax.axis_size(RING), lax.axis_size("dp")
    at = [(z % 2) * far + z // 2 for z in range(n)]
    return lax.ppermute(value, RING, [(at[z], at[(z + step) % n]) for z in range(n)])


def half_of(width):
    return (width // 256 + 1) // 2 * 256


def ring_gather(value):
    n = lax.axis_size(RING)
    got = {0: value}
    fore = back = value
    for step in range(1, n // 2):
        fore = shift(fore, 1)
        back = shift(back, -1)
        got[n - step] = fore
        got[step] = back
    half = half_of(value.shape[1])
    left = shift(fore[:, :half], 1)
    right = shift(back[:, half:], -1)
    return [got[i] for i in range(n) if i != n // 2] + [left, right]


def ring_scatter(far, near):
    bf, f32 = jnp.bfloat16, jnp.float32
    rows = far.shape[0] // 3
    half = half_of(far.shape[1])
    part = {i: far[(i - 3) * rows : (i - 2) * rows] for i in (3, 4, 5)}
    part |= {i: near[j * rows : (j + 1) * rows] for j, i in enumerate((0, 1, 2, 6, 7))}
    fore = shift(part[4][:, :half].astype(bf), 1).astype(f32)
    back = shift(part[4][:, half:].astype(bf), -1).astype(f32)
    fore = jnp.concatenate([part[3][:, :half] + fore, part[3][:, half:]], axis=1)
    back = jnp.concatenate([part[5][:, :half], part[5][:, half:] + back], axis=1)
    for step in (2, 1):
        fore = shift(fore.astype(bf), 1).astype(f32) + part[step]
        back = shift(back.astype(bf), -1).astype(f32) + part[8 - step]
    fore = shift(fore.astype(bf), 1).astype(f32)
    back = shift(back.astype(bf), -1).astype(f32)
    return (part[0] + fore + back).astype(bf)


def row_gather(same, other, share, z):
    units = lax.axis_size("dp")
    rest = same.shape[1] - units * share
    half = half_of(rest)

    def slice_for(i):
        part = same if i % 2 == 0 else other
        return lax.dynamic_slice_in_dim(part, rest + (z + i) % 8 // 2 * share, share, axis=1)

    cat = lambda *v: jnp.concatenate(v, axis=1)
    four = slice_for(4)
    hs = share // 2
    x1, x0 = other[:, :rest], same[:, :rest]
    fore1 = shift(cat(x1, slice_for(1), slice_for(3)), 1)
    back1 = shift(cat(x1, slice_for(7), slice_for(5)), -1)
    fore2 = shift(cat(x0, slice_for(2), four[:, :hs]), 2)
    back2 = shift(cat(x0, slice_for(6), four[:, hs:]), -2)
    full = rest + share
    fore3 = shift(cat(fore1[:, :rest], fore1[:, full:]), 2)
    back3 = shift(cat(back1[:, :rest], back1[:, full:]), -2)
    left = shift(cat(fore2[:, :half], fore2[:, full:]), 2)
    right = shift(cat(back2[:, half:rest], back2[:, full:]), -2)
    far = cat(left[:, :half], right[:, :-hs], left[:, half:], right[:, -hs:])
    own = cat(x0, slice_for(0))
    return [own, back1[:, :full], back2[:, :full], back3, far, fore3, fore2[:, :full], fore1[:, :full]]


def row_scatter(parts):
    bf, f32 = jnp.bfloat16, jnp.float32
    half = half_of(parts[0].shape[1])
    add = lambda u, v: (u.astype(f32) + v.astype(f32)).astype(bf)
    fore3, back3 = shift(parts[3], 2), shift(parts[5], -2)
    left, right = shift(parts[4][:, :half], 2), shift(parts[4][:, half:], -2)
    two = jnp.concatenate([add(parts[2][:, :half], left), parts[2][:, half:]], axis=1)
    six = jnp.concatenate([parts[6][:, :half], add(parts[6][:, half:], right)], axis=1)
    fore1, back1 = shift(add(parts[1], fore3), 1), shift(add(parts[7], back3), -1)
    fore2, back2 = shift(two, 2), shift(six, -2)
    same = parts[0].astype(f32) + fore2.astype(f32) + back2.astype(f32)
    return same.astype(bf), add(fore1, back1), fore3


def exchange(rows):
    n = lax.axis_size(PLANE)
    out = lax.all_to_all(rows.reshape(n, -1, rows.shape[1]), PLANE, 0, 0, tiled=True)
    return out.reshape(rows.shape)


def ranks(ids, own, rows):
    named = [ids[k][None, :] == own[:, None] for k in range(2)]
    member = (named[0] | named[1]).astype(jnp.bfloat16)
    before = (jnp.arange(rows)[:, None] < jnp.arange(rows)[None, :]).astype(jnp.bfloat16)
    rank = jnp.dot(member.reshape(-1, rows), before, preferred_element_type=jnp.float32)
    return named, rank.reshape(member.shape)


def own_slots(ids, own):
    named, rank = ranks(ids, own, ids.shape[1])
    hit = rank[:, None, :] == jnp.arange(8, dtype=jnp.float32)[None, :, None]
    return [
        (hit & named[k][:, None, :]).astype(jnp.bfloat16).reshape(-1, ids.shape[1])
        for k in range(2)
    ]


def dot(a, b):
    return jnp.dot(a, b, preferred_element_type=jnp.float32)


def dot_nt(a, b):
    return lax.dot_general(a, b, (((1,), (1,)), ((), ())), preferred_element_type=jnp.float32)


def dot_t(a, b):
    return lax.dot_general(a, b, (((0,), (0,)), ((), ())), preferred_element_type=jnp.float32)


def spread_kernel(split, own_ref, *refs):
    bf, f32 = jnp.bfloat16, jnp.float32
    *ids, id_left, left, right = refs[: 2 * 7 + 3]
    blocks, ids = ids[:7], ids[7:] + [id_left]
    out_ref, pick_ref = refs[2 * 7 + 3 :]
    rows = own_ref.shape[1]
    at = (0, 1, 2, 3, 5, 6, 7, 4)
    step = pl.program_id(0)

    @pl.when(step == 0)
    def _():
        own = own_ref[...]
        before = lax.broadcasted_iota(jnp.int32, (rows, rows), 0) < lax.broadcasted_iota(jnp.int32, (rows, rows), 1)
        before = before.astype(f32).astype(bf)
        slot = lax.broadcasted_iota(jnp.int32, (8 * CAP, rows), 0)
        for i, ref in zip(at, ids):
            named = ref[...].astype(f32).T
            member = (named[0:1] == own) | (named[1:2] == own)
            rank = dot(member.astype(f32).astype(bf), before)
            rank = jnp.where(member, rank, -1.0)
            wanted = jnp.where(slot % 8 == i, slot // 8, -2).astype(f32)
            hit = rank[:, None, :] == wanted[None]
            hit = jnp.where(hit, 1.0, 0.0).reshape(-1, rows)
            pick_ref[:, i * rows : (i + 1) * rows] = hit.astype(bf)

    far = jnp.where(step < split, left[...], right[...])
    vals = {i: ref[...] for i, ref in zip(at, blocks)}
    vals[4] = far
    vals = jnp.concatenate([vals[i] for i in range(8)], axis=0)
    out_ref[...] = dot(pick_ref[...], vals).astype(bf)


def spread(own, ring, cut):
    bf = jnp.bfloat16
    *blocks, left, right = ring
    rows = blocks[0].shape[0]
    tile = 256
    split = left.shape[1] // tile
    tail = (right.shape[1] - 128) // 128
    col = lambda f: pl.BlockSpec((rows, tile), lambda i: (0, f(i)))
    ids = lambda at: pl.BlockSpec((rows, 128), lambda i: (0, at))
    n = own.shape[0]
    body = functools.partial(spread_kernel, split)
    return pl.pallas_call(
        body,
        grid=(cut // tile,),
        in_specs=[pl.BlockSpec(own.shape, lambda i: (0, 0))]
        + [col(lambda i: i)] * 7
        + [ids(cut // 128)] * 7
        + [ids(tail), col(lambda i: jnp.minimum(i, split - 1)), col(lambda i: jnp.maximum(i - split, 0))],
        out_specs=[
            pl.BlockSpec((n * 8 * CAP, tile), lambda i: (0, i)),
            pl.BlockSpec((n * 8 * CAP, 8 * rows), lambda i: (0, 0)),
        ],
        out_shape=[
            jax.ShapeDtypeStruct((n * 8 * CAP, cut), bf),
            jax.ShapeDtypeStruct((n * 8 * CAP, 8 * rows), bf),
        ],
        compiler_params=pltpu.CompilerParams(vmem_limit_bytes=VMEM),
        cost_estimate=pl.CostEstimate(
            flops=2 * n * 8 * CAP * 8 * rows * cut, bytes_accessed=2 * n * 8 * CAP * 2 * cut, transcendentals=0
        ),
    )(own, *blocks, *blocks, right, left, right)


def grads_kernel(a_ref, b_ref, wg_ref, wu_ref, gate_ref, up_ref, back_ref):
    bf, f32 = jnp.bfloat16, jnp.float32
    cut = a_ref.shape[1]
    rest = wg_ref.shape[0] - cut
    gate_pre = dot(a_ref[...], wg_ref[:cut]) + dot(b_ref[:, :rest], wg_ref[cut:])
    up_pre = dot(a_ref[...], wu_ref[:cut]) + dot(b_ref[:, :rest], wu_ref[cut:])
    upstream = b_ref[:, rest:].astype(f32)
    sig = 1.0 / (1.0 + jnp.exp(-gate_pre))
    up_cot = (upstream * gate_pre * sig).astype(bf)
    gate_cot = (upstream * up_pre * sig * (1.0 + gate_pre * (1.0 - sig))).astype(bf)
    up_ref[...] = up_cot
    gate_ref[...] = gate_cot
    part = 256
    for lo in range(0, back_ref.shape[1], part):
        hi = min(lo + part, back_ref.shape[1])
        back_ref[:, lo:hi] = (dot_nt(gate_cot, wg_ref[lo:hi]) + dot_nt(up_cot, wu_ref[lo:hi])).astype(bf)


def local_grads(rows_a, rows_b, wg, wu, back):
    bf = jnp.bfloat16
    rows = rows_a.shape[0]
    width, share = wg.shape
    step = 256
    row = lambda n: pl.BlockSpec((step, n), lambda i: (i, 0))
    whole = pl.BlockSpec((width, share), lambda i: (0, 0))
    return pl.pallas_call(
        grads_kernel,
        grid=(rows // step,),
        in_specs=[row(rows_a.shape[1]), row(rows_b.shape[1]), whole, whole],
        out_specs=[row(share), row(share), row(back)],
        out_shape=[
            jax.ShapeDtypeStruct((rows, share), bf),
            jax.ShapeDtypeStruct((rows, share), bf),
            jax.ShapeDtypeStruct((rows, back), bf),
        ],
        compiler_params=pltpu.CompilerParams(vmem_limit_bytes=VMEM),
        cost_estimate=pl.CostEstimate(
            flops=4 * rows * share * (width + back), bytes_accessed=2 * rows * 2 * width, transcendentals=rows * share
        ),
    )(rows_a, rows_b, wg, wu)


def on_device(tokens, routes, hidden_grad, w_gate, w_up):
    bf, f32 = jnp.bfloat16, jnp.float32
    blocks, n = lax.axis_size(RING), lax.axis_size(PLANE)
    zl, zh = lax.axis_index("zl"), lax.axis_index("dp")
    x = tokens[0]
    tok, width = x.shape
    cut = width * CUT // 28
    rest = width - cut
    wg, wu = w_gate[0], w_up[0]
    share = wg.shape[1]
    le = jnp.arange(n)
    plane = (le // 8) * 16 + le % 8
    pair = jnp.stack([zl, 1 - zl])

    ids = routes[0].T
    lanes = jnp.pad(routes[0].astype(bf), ((0, 0), (0, 126)))
    ring = ring_gather(jnp.concatenate([x[:, :cut], lanes], axis=1))

    own0, own1 = own_slots(ids, (plane[:, None] + 8 * pair[None, :]).reshape(-1))
    own = own0 + own1
    grads = hidden_grad[0]
    near = jnp.concatenate(
        [dot(own, x[:, cut:]).astype(bf), (dot(own0, grads[:, 0]) + dot(own1, grads[:, 1])).astype(bf)],
        axis=1,
    )
    near = exchange(near).reshape(n, 2, 8, -1)[:, :, :CAP]
    near = near.transpose(1, 0, 2, 3).reshape(2, n * CAP, -1)

    near, ring = lax.optimization_barrier((near, ring))
    experts = jnp.broadcast_to((plane + zl * 8).astype(f32)[:, None], (n, tok))
    rows_a, pick = spread(experts, ring, cut)
    rows_a = exchange(rows_a)
    got = row_gather(near[0], near[1], share, zh * 2 + zl)
    got = jnp.stack(got, axis=1).reshape(n * CAP * blocks, -1)
    rows_b = got[:, :rest]

    cut = width * CUT_BACK // 28
    rest = width - cut
    gate_cot, up_cot, back_a = local_grads(rows_a, got, wg, wu, cut)
    back_a = exchange(back_a)

    def by_block(c):
        return c.reshape(n * CAP, blocks, share).transpose(1, 0, 2).reshape(-1, share)

    back_b = (dot_nt(by_block(gate_cot), wg[cut:]) + dot_nt(by_block(up_cot), wu[cut:])).astype(bf)
    back_b = back_b.reshape(blocks, n * CAP, rest)
    same, other, mark = row_scatter([back_b[i] for i in range(blocks)])

    def weight_grad(c):
        return jnp.concatenate([dot_t(rows_a, c).astype(bf), dot_t(rows_b, c).astype(bf)], axis=0)

    gate_cot, up_cot, pick, mark = lax.optimization_barrier((gate_cot, up_cot, pick, mark))
    grad_g, grad_u, spot = weight_grad(gate_cot), weight_grad(up_cot), pick.T
    back_a, same, other, grad_g, grad_u, spot = lax.optimization_barrier((back_a, same, other, grad_g, grad_u, spot))

    far = dot(spot[3 * tok : 6 * tok], back_a)
    back_a, far = lax.optimization_barrier((back_a, far))
    near = dot(jnp.concatenate([spot[: 3 * tok], spot[6 * tok :]], axis=0), back_a)
    grad_a = ring_scatter(far, near)
    back_b = jnp.stack([same.reshape(n, CAP, rest), other.reshape(n, CAP, rest)], axis=1)
    back_b = exchange(jnp.pad(back_b, ((0, 0), (0, 0), (0, 8 - CAP), (0, 0))).reshape(-1, rest))
    grad_b = dot_t(own, back_b).astype(bf)
    token_grad = jnp.concatenate([grad_a, grad_b], axis=1)
    return token_grad[None], grad_g[None], grad_u[None]


def solution(mesh):
    fine = Mesh(mesh.devices.reshape(4, 2, 4, 2, 4), ("x", "zl", "y", "core", "dp"))
    return jax.shard_map(
        on_device,
        mesh=fine,
        in_specs=(
            P("dp", EXPERT, None),
            P("dp", EXPERT, None),
            P("dp", EXPERT, None, None),
            P(EXPERT, None, "dp"),
            P(EXPERT, None, "dp"),
        ),
        out_specs=(P("dp", EXPERT, None), P(EXPERT, None, "dp"), P(EXPERT, None, "dp")),
        check_vma=False,
    )
```

```python
import functools

import jax
import jax.numpy as jnp
from jax import lax
from jax.experimental import pallas as pl
from jax.experimental.pallas import tpu as pltpu
from jax.sharding import Mesh, PartitionSpec as P

RING = ("zl", "dp")
PLANE = ("x", "y", "core")
EXPERT = ("x", "zl", "y", "core")
CAP = 5
VMEM = 56 * 2**20
CUT = 18
CUT_BACK = 18


def shift(value, step):
    n, far = lax.axis_size(RING), lax.axis_size("dp")
    at = [(z % 2) * far + z // 2 for z in range(n)]
    return lax.ppermute(value, RING, [(at[z], at[(z + step) % n]) for z in range(n)])


def half_of(width):
    return (width // 256 + 1) // 2 * 256


def ring_gather(value):
    n = lax.axis_size(RING)
    got = {0: value}
    fore = back = value
    for step in range(1, n // 2):
        fore = shift(fore, 1)
        back = shift(back, -1)
        got[n - step] = fore
        got[step] = back
    half = half_of(value.shape[1])
    left = shift(fore[:, :half], 1)
    right = shift(back[:, half:], -1)
    return [got[i] for i in range(n) if i != n // 2] + [left, right], got[1]


def ring_scatter(far, near):
    bf, f32 = jnp.bfloat16, jnp.float32
    rows = far.shape[0]
    half = half_of(far.shape[1])
    part = {i: near[j * rows : (j + 1) * rows] for j, i in enumerate((0, 1, 2, 3, 5, 6, 7))}
    fore = shift(far[:, :half].astype(bf), 1).astype(f32)
    back = shift(far[:, half:].astype(bf), -1).astype(f32)
    fore = jnp.concatenate([part[3][:, :half] + fore, part[3][:, half:]], axis=1)
    back = jnp.concatenate([part[5][:, :half], part[5][:, half:] + back], axis=1)
    for step in (2, 1):
        fore = shift(fore.astype(bf), 1).astype(f32) + part[step]
        back = shift(back.astype(bf), -1).astype(f32) + part[8 - step]
    fore = shift(fore.astype(bf), 1).astype(f32)
    back = shift(back.astype(bf), -1).astype(f32)
    return (part[0] + fore + back).astype(bf)


def row_gather(same, other, share, z):
    units = lax.axis_size("dp")
    rest = same.shape[1] - units * share
    half = half_of(rest)

    def slice_for(i):
        part = same if i % 2 == 0 else other
        return lax.dynamic_slice_in_dim(part, rest + (z + i) % 8 // 2 * share, share, axis=1)

    cat = lambda *v: jnp.concatenate(v, axis=1)
    four = slice_for(4)
    hs = share // 2
    x1, x0 = other[:, :rest], same[:, :rest]
    fore1 = shift(cat(x1, slice_for(1), slice_for(3)), 1)
    back1 = shift(cat(x1, slice_for(7), slice_for(5)), -1)
    fore2 = shift(cat(x0, slice_for(2), four[:, :hs]), 2)
    back2 = shift(cat(x0, slice_for(6), four[:, hs:]), -2)
    full = rest + share
    fore3 = shift(cat(fore1[:, :rest], fore1[:, full:]), 2)
    back3 = shift(cat(back1[:, :rest], back1[:, full:]), -2)
    left = shift(cat(fore2[:, :half], fore2[:, full:]), 2)
    right = shift(cat(back2[:, half:rest], back2[:, full:]), -2)
    far = cat(left[:, :half], right[:, :-hs], left[:, half:], right[:, -hs:])
    own = cat(x0, slice_for(0))
    return [own, back1[:, :full], back2[:, :full], back3, far, fore3, fore2[:, :full], fore1[:, :full]]


def row_scatter(parts):
    bf, f32 = jnp.bfloat16, jnp.float32
    half = half_of(parts[0].shape[1])
    add = lambda u, v: (u.astype(f32) + v.astype(f32)).astype(bf)
    fore3, back3 = shift(parts[3], 2), shift(parts[5], -2)
    left, right = shift(parts[4][:, :half], 2), shift(parts[4][:, half:], -2)
    two = jnp.concatenate([add(parts[2][:, :half], left), parts[2][:, half:]], axis=1)
    six = jnp.concatenate([parts[6][:, :half], add(parts[6][:, half:], right)], axis=1)
    fore1, back1 = shift(add(parts[1], fore3), 1), shift(add(parts[7], back3), -1)
    fore2, back2 = shift(two, 2), shift(six, -2)
    same = parts[0].astype(f32) + fore2.astype(f32) + back2.astype(f32)
    return same.astype(bf), add(fore1, back1), fore3


def exchange(rows):
    n = lax.axis_size(PLANE)
    out = lax.all_to_all(rows.reshape(n, -1, rows.shape[1]), PLANE, 0, 0, tiled=True)
    return out.reshape(rows.shape)


def ranks(ids, own, rows):
    named = [ids[k][None, :] == own[:, None] for k in range(2)]
    member = (named[0] | named[1]).astype(jnp.bfloat16)
    before = (jnp.arange(rows)[:, None] < jnp.arange(rows)[None, :]).astype(jnp.bfloat16)
    rank = jnp.dot(member.reshape(-1, rows), before, preferred_element_type=jnp.float32)
    return named, rank.reshape(member.shape)


def own_slots(ids, own):
    named, rank = ranks(ids, own, ids.shape[1])
    hit = rank[:, None, :] == jnp.arange(8, dtype=jnp.float32)[None, :, None]
    return [
        (hit & named[k][:, None, :]).astype(jnp.bfloat16).reshape(-1, ids.shape[1])
        for k in range(2)
    ]


def dot(a, b):
    return jnp.dot(a, b, preferred_element_type=jnp.float32)


def dot_nt(a, b):
    return lax.dot_general(a, b, (((1,), (1,)), ((), ())), preferred_element_type=jnp.float32)


def dot_t(a, b):
    return lax.dot_general(a, b, (((0,), (0,)), ((), ())), preferred_element_type=jnp.float32)


def spread_kernel(split, own_ref, *refs):
    bf, f32 = jnp.bfloat16, jnp.float32
    *ids, id_left, left, right = refs[: 2 * 7 + 3]
    blocks, ids = ids[:7], ids[7:] + [id_left]
    out_ref, pick_ref = refs[2 * 7 + 3 :]
    rows = own_ref.shape[1]
    at = (0, 1, 2, 3, 5, 6, 7, 4)
    step = pl.program_id(0)

    @pl.when(step == 0)
    def _():
        own = own_ref[...]
        before = lax.broadcasted_iota(jnp.int32, (rows, rows), 0) < lax.broadcasted_iota(jnp.int32, (rows, rows), 1)
        before = before.astype(f32).astype(bf)
        slot = lax.broadcasted_iota(jnp.int32, (8 * CAP, rows), 0)
        for i, ref in zip(at, ids):
            named = ref[...].astype(f32).T
            member = (named[0:1] == own) | (named[1:2] == own)
            rank = dot(member.astype(f32).astype(bf), before)
            rank = jnp.where(member, rank, -1.0)
            wanted = jnp.where(slot % 8 == i, slot // 8, -2).astype(f32)
            hit = rank[:, None, :] == wanted[None]
            hit = jnp.where(hit, 1.0, 0.0).reshape(-1, rows)
            pick_ref[:, i * rows : (i + 1) * rows] = hit.astype(bf)

    far = jnp.where(step < split, left[...], right[...])
    vals = {i: ref[...] for i, ref in zip(at, blocks)}
    vals[4] = far
    vals = jnp.concatenate([vals[i] for i in range(8)], axis=0)
    out_ref[...] = dot(pick_ref[...], vals).astype(bf)


def spread(own, ring, cut):
    bf = jnp.bfloat16
    *blocks, left, right = ring
    rows = blocks[0].shape[0]
    tile = 256
    split = left.shape[1] // tile
    tail = (right.shape[1] - 128) // 128
    col = lambda f: pl.BlockSpec((rows, tile), lambda i: (0, f(i)))
    ids = lambda at: pl.BlockSpec((rows, 128), lambda i: (0, at))
    n = own.shape[0]
    body = functools.partial(spread_kernel, split)
    return pl.pallas_call(
        body,
        grid=(cut // tile,),
        in_specs=[pl.BlockSpec(own.shape, lambda i: (0, 0))]
        + [col(lambda i: i)] * 7
        + [ids(cut // 128)] * 7
        + [ids(tail), col(lambda i: jnp.minimum(i, split - 1)), col(lambda i: jnp.maximum(i - split, 0))],
        out_specs=[
            pl.BlockSpec((n * 8 * CAP, tile), lambda i: (0, i)),
            pl.BlockSpec((n * 8 * CAP, 8 * rows), lambda i: (0, 0)),
        ],
        out_shape=[
            jax.ShapeDtypeStruct((n * 8 * CAP, cut), bf),
            jax.ShapeDtypeStruct((n * 8 * CAP, 8 * rows), bf),
        ],
        compiler_params=pltpu.CompilerParams(vmem_limit_bytes=VMEM),
        cost_estimate=pl.CostEstimate(
            flops=2 * n * 8 * CAP * 8 * rows * cut, bytes_accessed=2 * n * 8 * CAP * 2 * cut, transcendentals=0
        ),
    )(own, *blocks, *blocks, right, left, right)


def grads_kernel(a_ref, b_ref, wg_ref, wu_ref, gate_ref, up_ref, back_ref, block_ref, wide_ref):
    bf, f32 = jnp.bfloat16, jnp.float32
    cut = a_ref.shape[1]
    rest = wg_ref.shape[0] - cut
    gate_pre = dot(a_ref[...], wg_ref[:cut]) + dot(b_ref[:, :rest], wg_ref[cut:])
    up_pre = dot(a_ref[...], wu_ref[:cut]) + dot(b_ref[:, :rest], wu_ref[cut:])
    upstream = b_ref[:, rest:].astype(f32)
    sig = 1.0 / (1.0 + jnp.exp(-gate_pre))
    up_cot = (upstream * gate_pre * sig).astype(bf)
    gate_cot = (upstream * up_pre * sig * (1.0 + gate_pre * (1.0 - sig))).astype(bf)
    up_ref[...] = up_cot
    gate_ref[...] = gate_cot
    part = 256
    for lo in range(0, back_ref.shape[1], part):
        hi = min(lo + part, back_ref.shape[1])
        back_ref[:, lo:hi] = (dot_nt(gate_cot, wg_ref[lo:hi]) + dot_nt(up_cot, wu_ref[lo:hi])).astype(bf)
    cut = back_ref.shape[1]
    blocks, rows, rest = block_ref.shape

    def by_block(c):
        c = c.astype(f32)
        for t in range(c.shape[1] // 128):
            wide_ref[t] = c[:, t * 128 : (t + 1) * 128]
        return jnp.concatenate(
            [
                jnp.concatenate([wide_ref[t, pl.ds(i, rows, stride=blocks), :] for t in range(c.shape[1] // 128)], axis=1)
                for i in range(blocks)
            ],
            axis=0,
        ).astype(bf)

    gate_cot, up_cot = by_block(gate_cot), by_block(up_cot)
    for lo in range(0, rest, part):
        hi = min(lo + part, rest)
        at = slice(cut + lo, cut + hi)
        wide = (dot_nt(gate_cot, wg_ref[at]) + dot_nt(up_cot, wu_ref[at])).astype(bf)
        block_ref[:, :, lo:hi] = wide.reshape(blocks, rows, hi - lo)


def local_grads(rows_a, rows_b, wg, wu, back):
    bf = jnp.bfloat16
    rows = rows_a.shape[0]
    width, share = wg.shape
    step = 256
    row = lambda n: pl.BlockSpec((step, n), lambda i: (i, 0))
    whole = pl.BlockSpec((width, share), lambda i: (0, 0))
    return pl.pallas_call(
        grads_kernel,
        grid=(rows // step,),
        in_specs=[row(rows_a.shape[1]), row(rows_b.shape[1]), whole, whole],
        out_specs=[
            row(share),
            row(share),
            row(back),
            pl.BlockSpec((8, step // 8, width - back), lambda i: (0, i, 0)),
        ],
        out_shape=[
            jax.ShapeDtypeStruct((rows, share), bf),
            jax.ShapeDtypeStruct((rows, share), bf),
            jax.ShapeDtypeStruct((rows, back), bf),
            jax.ShapeDtypeStruct((8, rows // 8, width - back), bf),
        ],
        scratch_shapes=[pltpu.VMEM((share // 128, step, 128), jnp.float32)],
        compiler_params=pltpu.CompilerParams(vmem_limit_bytes=VMEM),
        cost_estimate=pl.CostEstimate(
            flops=8 * rows * share * width, bytes_accessed=2 * rows * 2 * width, transcendentals=rows * share
        ),
    )(rows_a, rows_b, wg, wu)


def on_device(tokens, routes, hidden_grad, w_gate, w_up):
    bf, f32 = jnp.bfloat16, jnp.float32
    blocks, n = lax.axis_size(RING), lax.axis_size(PLANE)
    zl, zh = lax.axis_index("zl"), lax.axis_index("dp")
    x = tokens[0]
    tok, width = x.shape
    cut = width * CUT // 28
    rest = width - cut
    wg, wu = w_gate[0], w_up[0]
    share = wg.shape[1]
    le = jnp.arange(n)
    plane = (le // 8) * 16 + le % 8
    pair = jnp.stack([zl, 1 - zl])

    ids = routes[0].T
    lanes = jnp.pad(routes[0].astype(bf), ((0, 0), (0, 126)))
    ring, mark = ring_gather(jnp.concatenate([x[:, :cut], lanes], axis=1))

    own0, own1 = own_slots(ids, (plane[:, None] + 8 * pair[None, :]).reshape(-1))
    own = own0 + own1
    x_b, grads, mark = lax.optimization_barrier((x[:, cut:], hidden_grad[0], mark))
    near = jnp.concatenate(
        [dot(own, x_b).astype(bf), (dot(own0, grads[:, 0]) + dot(own1, grads[:, 1])).astype(bf)],
        axis=1,
    )
    near = exchange(near).reshape(n, 2, 8, -1)[:, :, :CAP]
    near = near.transpose(1, 0, 2, 3).reshape(2, n * CAP, -1)

    experts = jnp.broadcast_to((plane + zl * 8).astype(f32)[:, None], (n, tok))
    rows_a, pick = spread(experts, ring, cut)
    rows_a, near = lax.optimization_barrier((rows_a, near))
    rows_a = exchange(rows_a)
    got = row_gather(near[0], near[1], share, zh * 2 + zl)
    got = jnp.stack(got, axis=1).reshape(n * CAP * blocks, -1)
    rows_b = got[:, :rest]

    cut = width * CUT_BACK // 28
    rest = width - cut
    gate_cot, up_cot, back_a, back_b = local_grads(rows_a, got, wg, wu, cut)
    back_a = exchange(back_a)

    same, other, mark = row_scatter([back_b[i] for i in range(blocks)])

    def weight_grad(c):
        return jnp.concatenate([dot_t(rows_a, c).astype(bf), dot_t(rows_b, c).astype(bf)], axis=0)

    gate_cot, up_cot, pick, mark = lax.optimization_barrier((gate_cot, up_cot, pick, mark))
    grad_g, grad_u = weight_grad(gate_cot), weight_grad(up_cot)
    spot4 = pick[:, 4 * tok : 5 * tok].T
    spots = jnp.concatenate([pick[:, : 4 * tok], pick[:, 5 * tok :]], axis=1).T
    back_a, same, other, grad_g, grad_u, spot4, spots = lax.optimization_barrier(
        (back_a, same, other, grad_g, grad_u, spot4, spots)
    )

    far = dot(spot4, back_a)
    back_a, far = lax.optimization_barrier((back_a, far))
    near = dot(spots, back_a)
    grad_a = ring_scatter(far, near)
    back_b = jnp.stack([same.reshape(n, CAP, rest), other.reshape(n, CAP, rest)], axis=1)
    back_b = exchange(jnp.pad(back_b, ((0, 0), (0, 0), (0, 8 - CAP), (0, 0))).reshape(-1, rest))
    grad_b = dot_t(own, back_b).astype(bf)
    token_grad = jnp.concatenate([grad_a, grad_b], axis=1)
    return token_grad[None], grad_g[None], grad_u[None]


def solution(mesh):
    fine = Mesh(mesh.devices.reshape(4, 2, 4, 2, 4), ("x", "zl", "y", "core", "dp"))
    return jax.shard_map(
        on_device,
        mesh=fine,
        in_specs=(
            P("dp", EXPERT, None),
            P("dp", EXPERT, None),
            P("dp", EXPERT, None, None),
            P(EXPERT, None, "dp"),
            P(EXPERT, None, "dp"),
        ),
        out_specs=(P("dp", EXPERT, None), P(EXPERT, None, "dp"), P(EXPERT, None, "dp")),
        check_vma=False,
    )
```

```python
import jax
import jax.numpy as jnp
from jax import lax
from jax.experimental import pallas as pl
from jax.experimental.pallas import tpu as pltpu
from jax.sharding import Mesh, PartitionSpec as P

RING = ("zl", "dp")
PLANE = ("x", "y", "core")
EXPERT = ("x", "zl", "y", "core")
CAP = 5
VMEM = 56 * 2**20
CUT = 18
CUT_BACK = 18


def shift(value, step):
    n, far = lax.axis_size(RING), lax.axis_size("dp")
    at = [(z % 2) * far + z // 2 for z in range(n)]
    return lax.ppermute(value, RING, [(at[z], at[(z + step) % n]) for z in range(n)])


def half_of(width):
    return (width // 256 + 1) // 2 * 256


def ring_gather(value):
    n = lax.axis_size(RING)
    got = {0: value}
    fore = back = value
    for step in range(1, n // 2):
        fore = shift(fore, 1)
        back = shift(back, -1)
        got[n - step] = fore
        got[step] = back
    half = half_of(value.shape[1])
    left = shift(fore[:, :half], 1)
    right = shift(back[:, half:], -1)
    return [got[i] for i in range(n) if i != n // 2] + [left, right]


def ring_scatter(far, near):
    bf, f32 = jnp.bfloat16, jnp.float32
    rows = far.shape[0] // 3
    half = half_of(far.shape[1])
    part = {i: far[(i - 3) * rows : (i - 2) * rows] for i in (3, 4, 5)}
    left = shift(part[4][:, :half].astype(bf), 1)
    right = shift(part[4][:, half:].astype(bf), -1)
    fore = jnp.concatenate([part[3][:, :half] + left.astype(f32), part[3][:, half:]], axis=1).astype(bf)
    back = jnp.concatenate([part[5][:, :half], part[5][:, half:] + right.astype(f32)], axis=1).astype(bf)
    near = near((fore, back))
    part |= {i: near[j * rows : (j + 1) * rows] for j, i in enumerate((0, 1, 2, 6, 7))}
    for step in (2, 1):
        fore = (shift(fore, 1).astype(f32) + part[step]).astype(bf)
        back = (shift(back, -1).astype(f32) + part[8 - step]).astype(bf)
    fore = shift(fore, 1).astype(f32)
    back = shift(back, -1).astype(f32)
    return (part[0] + fore + back).astype(bf)


def row_gather(same, other, share, z):
    units = lax.axis_size("dp")
    rest = same.shape[1] - units * share
    half = half_of(rest)

    def slice_for(i):
        part = same if i % 2 == 0 else other
        return lax.dynamic_slice_in_dim(part, rest + (z + i) % 8 // 2 * share, share, axis=1)

    cat = lambda *v: jnp.concatenate(v, axis=1)
    four = slice_for(4)
    hs = share // 2
    x1, x0 = other[:, :rest], same[:, :rest]
    fore1 = shift(cat(x1, slice_for(1), slice_for(3)), 1)
    back1 = shift(cat(x1, slice_for(7), slice_for(5)), -1)
    fore2 = shift(cat(x0, slice_for(2), four[:, :hs]), 2)
    back2 = shift(cat(x0, slice_for(6), four[:, hs:]), -2)
    full = rest + share
    fore3 = shift(cat(fore1[:, :rest], fore1[:, full:]), 2)
    back3 = shift(cat(back1[:, :rest], back1[:, full:]), -2)
    left = shift(cat(fore2[:, :half], fore2[:, full:]), 2)
    right = shift(cat(back2[:, half:rest], back2[:, full:]), -2)
    far = cat(left[:, :half], right[:, :-hs], left[:, half:], right[:, -hs:])
    own = cat(x0, slice_for(0))
    return [own, back1[:, :full], back2[:, :full], back3, far, fore3, fore2[:, :full], fore1[:, :full]]


def row_scatter(parts, beside):
    bf, f32 = jnp.bfloat16, jnp.float32
    half = half_of(parts[0].shape[1])
    add = lambda u, v: (u.astype(f32) + v.astype(f32)).astype(bf)
    fore3, back3 = shift(parts[3], 2), shift(parts[5], -2)
    left, right = shift(parts[4][:, :half], 2), shift(parts[4][:, half:], -2)
    fore3, back3, beside = lax.optimization_barrier((fore3, back3, beside((left, right))))
    two = jnp.concatenate([add(parts[2][:, :half], left), parts[2][:, half:]], axis=1)
    six = jnp.concatenate([parts[6][:, :half], add(parts[6][:, half:], right)], axis=1)
    one, seven = add(parts[1], fore3), add(parts[7], back3)
    fore1, back1 = shift(one, 1), shift(seven, -1)
    fore2, back2 = shift(two, 2), shift(six, -2)
    fore1, back1, fore2, back2 = lax.optimization_barrier((fore1, back1, fore2, back2))
    same = parts[0].astype(f32) + fore2.astype(f32) + back2.astype(f32)
    return same.astype(bf), add(fore1, back1), beside


def exchange(rows):
    n = lax.axis_size(PLANE)
    out = lax.all_to_all(rows.reshape(n, -1, rows.shape[1]), PLANE, 0, 0, tiled=True)
    return out.reshape(rows.shape)


def ranks(ids, own, rows):
    named = [ids[k][None, :] == own[:, None] for k in range(2)]
    member = (named[0] | named[1]).astype(jnp.bfloat16)
    before = (jnp.arange(rows)[:, None] < jnp.arange(rows)[None, :]).astype(jnp.bfloat16)
    rank = jnp.dot(member.reshape(-1, rows), before, preferred_element_type=jnp.float32)
    return named, rank.reshape(member.shape)


def own_slots(ids, own):
    named, rank = ranks(ids, own, ids.shape[1])
    hit = rank[:, None, :] == jnp.arange(8, dtype=jnp.float32)[None, :, None]
    return [
        (hit & named[k][:, None, :]).astype(jnp.bfloat16).reshape(-1, ids.shape[1])
        for k in range(2)
    ]


def dot(a, b):
    return jnp.dot(a, b, preferred_element_type=jnp.float32)


def dot_nt(a, b):
    return lax.dot_general(a, b, (((1,), (1,)), ((), ())), preferred_element_type=jnp.float32)


def dot_t(a, b):
    return lax.dot_general(a, b, (((0,), (0,)), ((), ())), preferred_element_type=jnp.float32)


def spread_kernel(own_ref, *refs):
    bf, f32 = jnp.bfloat16, jnp.float32
    *ids, id_left, left, right = refs[: 2 * 7 + 3]
    blocks, ids = ids[:7], ids[7:] + [id_left]
    out_ref, pick_ref, far_ref = refs[2 * 7 + 3 :]
    split = left.shape[1]
    tile = out_ref.shape[1]
    rows = own_ref.shape[1]
    at = (0, 1, 2, 3, 5, 6, 7, 4)
    step = pl.program_id(0)

    @pl.when(step == 0)
    def _():
        far_ref[:, :split] = left[...]
        far_ref[:, split:] = right[:, : far_ref.shape[1] - split]
        own = own_ref[...]
        before = lax.broadcasted_iota(jnp.int32, (rows, rows), 0) < lax.broadcasted_iota(jnp.int32, (rows, rows), 1)
        before = before.astype(f32).astype(bf)
        slot = lax.broadcasted_iota(jnp.int32, (8 * CAP, rows), 0)
        for i, ref in zip(at, ids):
            named = ref[...].astype(f32).T
            member = (named[0:1] == own) | (named[1:2] == own)
            rank = dot(member.astype(f32).astype(bf), before)
            rank = jnp.where(member, rank, -1.0)
            wanted = jnp.where(slot % 8 == i, slot // 8, -2).astype(f32)
            hit = rank[:, None, :] == wanted[None]
            hit = jnp.where(hit, 1.0, 0.0).reshape(-1, rows)
            pick_ref[:, i * rows : (i + 1) * rows] = hit.astype(bf)

    vals = {i: ref[...] for i, ref in zip(at, blocks)}
    vals[4] = far_ref[:, pl.ds(pl.multiple_of(step * tile, 128), tile)]
    vals = jnp.concatenate([vals[i] for i in range(8)], axis=0)
    out_ref[...] = dot(pick_ref[...], vals).astype(bf)


def spread(own, ring, cut):
    bf = jnp.bfloat16
    *blocks, left, right = ring
    rows = blocks[0].shape[0]
    tile = 768
    tail = (right.shape[1] - 128) // 128
    col = lambda f: pl.BlockSpec((rows, tile), lambda i: (0, f(i)))
    ids = lambda at: pl.BlockSpec((rows, 128), lambda i: (0, at))
    n = own.shape[0]
    whole = lambda v: pl.BlockSpec(v.shape, lambda i: (0, 0))
    return pl.pallas_call(
        spread_kernel,
        grid=(cut // tile,),
        in_specs=[pl.BlockSpec(own.shape, lambda i: (0, 0))]
        + [col(lambda i: i)] * 7
        + [ids(cut // 128)] * 7
        + [ids(tail), whole(left), whole(right)],
        out_specs=[
            pl.BlockSpec((n * 8 * CAP, tile), lambda i: (0, i)),
            pl.BlockSpec((n * 8 * CAP, 8 * rows), lambda i: (0, 0)),
        ],
        out_shape=[
            jax.ShapeDtypeStruct((n * 8 * CAP, cut), bf),
            jax.ShapeDtypeStruct((n * 8 * CAP, 8 * rows), bf),
        ],
        scratch_shapes=[pltpu.VMEM((rows, cut), bf)],
        compiler_params=pltpu.CompilerParams(vmem_limit_bytes=VMEM),
        cost_estimate=pl.CostEstimate(
            flops=2 * n * 8 * CAP * 8 * rows * cut, bytes_accessed=2 * n * 8 * CAP * 2 * cut, transcendentals=0
        ),
    )(own, *blocks, *blocks, right, left, right)


def grads_kernel(a_ref, b_ref, wg_ref, wu_ref, gate_ref, up_ref, back_ref, block_ref, wide_ref):
    bf, f32 = jnp.bfloat16, jnp.float32
    cut = a_ref.shape[1]
    rest = wg_ref.shape[0] - cut
    gate_pre = dot(a_ref[...], wg_ref[:cut]) + dot(b_ref[:, :rest], wg_ref[cut:])
    up_pre = dot(a_ref[...], wu_ref[:cut]) + dot(b_ref[:, :rest], wu_ref[cut:])
    upstream = b_ref[:, rest:].astype(f32)
    sig = 1.0 / (1.0 + jnp.exp(-gate_pre))
    up_cot = (upstream * gate_pre * sig).astype(bf)
    gate_cot = (upstream * up_pre * sig * (1.0 + gate_pre * (1.0 - sig))).astype(bf)
    up_ref[...] = up_cot
    gate_ref[...] = gate_cot
    part = 256
    for lo in range(0, back_ref.shape[1], part):
        hi = min(lo + part, back_ref.shape[1])
        back_ref[:, lo:hi] = (dot_nt(gate_cot, wg_ref[lo:hi]) + dot_nt(up_cot, wu_ref[lo:hi])).astype(bf)
    cut = back_ref.shape[1]
    blocks, rows, rest = block_ref.shape

    def by_block(c):
        c = c.astype(f32)
        for t in range(c.shape[1] // 128):
            wide_ref[t] = c[:, t * 128 : (t + 1) * 128]
        return jnp.concatenate(
            [
                jnp.concatenate([wide_ref[t, pl.ds(i, rows, stride=blocks), :] for t in range(c.shape[1] // 128)], axis=1)
                for i in range(blocks)
            ],
            axis=0,
        ).astype(bf)

    gate_cot, up_cot = by_block(gate_cot), by_block(up_cot)
    for lo in range(0, rest, part):
        hi = min(lo + part, rest)
        at = slice(cut + lo, cut + hi)
        wide = (dot_nt(gate_cot, wg_ref[at]) + dot_nt(up_cot, wu_ref[at])).astype(bf)
        block_ref[:, :, lo:hi] = wide.reshape(blocks, rows, hi - lo)


def local_grads(rows_a, rows_b, wg, wu, back):
    bf = jnp.bfloat16
    rows = rows_a.shape[0]
    width, share = wg.shape
    step = 256
    row = lambda n: pl.BlockSpec((step, n), lambda i: (i, 0))
    whole = pl.BlockSpec((width, share), lambda i: (0, 0))
    return pl.pallas_call(
        grads_kernel,
        grid=(rows // step,),
        in_specs=[row(rows_a.shape[1]), row(rows_b.shape[1]), whole, whole],
        out_specs=[
            row(share),
            row(share),
            row(back),
            pl.BlockSpec((8, step // 8, width - back), lambda i: (0, i, 0)),
        ],
        out_shape=[
            jax.ShapeDtypeStruct((rows, share), bf),
            jax.ShapeDtypeStruct((rows, share), bf),
            jax.ShapeDtypeStruct((rows, back), bf),
            jax.ShapeDtypeStruct((8, rows // 8, width - back), bf),
        ],
        scratch_shapes=[pltpu.VMEM((share // 128, step, 128), jnp.float32)],
        compiler_params=pltpu.CompilerParams(vmem_limit_bytes=VMEM),
        cost_estimate=pl.CostEstimate(
            flops=8 * rows * share * width, bytes_accessed=2 * rows * 2 * width, transcendentals=rows * share
        ),
    )(rows_a, rows_b, wg, wu)


def on_device(tokens, routes, hidden_grad, w_gate, w_up):
    bf, f32 = jnp.bfloat16, jnp.float32
    blocks, n = lax.axis_size(RING), lax.axis_size(PLANE)
    zl, zh = lax.axis_index("zl"), lax.axis_index("dp")
    x = tokens[0]
    tok, width = x.shape
    cut = width * CUT // 28
    rest = width - cut
    wg, wu = w_gate[0], w_up[0]
    share = wg.shape[1]
    le = jnp.arange(n)
    plane = (le // 8) * 16 + le % 8
    pair = jnp.stack([zl, 1 - zl])

    ids = routes[0].T
    lanes = jnp.pad(routes[0].astype(bf), ((0, 0), (0, 126)))
    ring = ring_gather(jnp.concatenate([x[:, :cut], lanes], axis=1))

    own0, own1 = own_slots(ids, (plane[:, None] + 8 * pair[None, :]).reshape(-1))
    own = own0 + own1
    x_b, grads = x[:, cut:], hidden_grad[0]
    near = jnp.concatenate(
        [dot(own, x_b).astype(bf), (dot(own0, grads[:, 0]) + dot(own1, grads[:, 1])).astype(bf)],
        axis=1,
    )
    near = exchange(near)

    experts = jnp.broadcast_to((plane + zl * 8).astype(f32)[:, None], (n, tok))
    rows_a, pick = spread(experts, ring, cut)
    rows_a, near = lax.optimization_barrier((rows_a, near))
    rows_a = exchange(rows_a)
    near = near.reshape(n, 2, 8, -1)[:, :, :CAP].transpose(1, 0, 2, 3).reshape(2, n * CAP, -1)
    got = row_gather(near[0], near[1], share, zh * 2 + zl)
    got = jnp.stack(got, axis=1).reshape(n * CAP * blocks, -1)
    rows_b = got[:, :rest]

    cut = width * CUT_BACK // 28
    rest = width - cut
    gate_cot, up_cot, back_a, back_b = local_grads(rows_a, got, wg, wu, cut)
    back_a = exchange(back_a)

    def weight_grads(mark):
        cots, _ = lax.optimization_barrier(((gate_cot, up_cot), mark))
        return [
            jnp.concatenate([dot_t(rows_a, c).astype(bf), dot_t(rows_b, c).astype(bf)], axis=0) for c in cots
        ]

    spot_far = pick[:, 3 * tok : 6 * tok].T
    spot_near = jnp.concatenate([pick[:, : 3 * tok], pick[:, 6 * tok :]], axis=1).T
    same, other, (grad_g, grad_u) = row_scatter([back_b[i] for i in range(blocks)], weight_grads)
    back_a, same, other, spot_far, spot_near = lax.optimization_barrier((back_a, same, other, spot_far, spot_near))

    grad_a = ring_scatter(
        dot(spot_far, back_a), lambda mark: dot(spot_near, lax.optimization_barrier((back_a, mark))[0])
    )
    back_b = jnp.stack([same.reshape(n, CAP, rest), other.reshape(n, CAP, rest)], axis=1)
    back_b = exchange(jnp.pad(back_b, ((0, 0), (0, 0), (0, 8 - CAP), (0, 0))).reshape(-1, rest))
    grad_b = dot_t(own, back_b).astype(bf)
    token_grad = jnp.concatenate([grad_a, grad_b], axis=1)
    return token_grad[None], grad_g[None], grad_u[None]


def solution(mesh):
    fine = Mesh(mesh.devices.reshape(4, 2, 4, 2, 4), ("x", "zl", "y", "core", "dp"))
    return jax.shard_map(
        on_device,
        mesh=fine,
        in_specs=(
            P("dp", EXPERT, None),
            P("dp", EXPERT, None),
            P("dp", EXPERT, None, None),
            P(EXPERT, None, "dp"),
            P(EXPERT, None, "dp"),
        ),
        out_specs=(P("dp", EXPERT, None), P(EXPERT, None, "dp"), P(EXPERT, None, "dp")),
        check_vma=False,
    )
```

```python
import jax
import jax.numpy as jnp
from jax import lax
from jax.experimental import pallas as pl
from jax.experimental.pallas import tpu as pltpu
from jax.sharding import Mesh, PartitionSpec as P

RING = ("zl", "dp")
PLANE = ("x", "y", "core")
EXPERT = ("x", "zl", "y", "core")
CAP = 5
VMEM = 56 * 2**20
CUT = 18
CUT_BACK = 18


def shift(value, step):
    n, far = lax.axis_size(RING), lax.axis_size("dp")
    at = [(z % 2) * far + z // 2 for z in range(n)]
    return lax.ppermute(value, RING, [(at[z], at[(z + step) % n]) for z in range(n)])


def half_of(width):
    return (width // 256 + 1) // 2 * 256


def ring_gather(value):
    n = lax.axis_size(RING)
    got = {0: value}
    fore = back = value
    for step in range(1, n // 2):
        fore = shift(fore, 1)
        back = shift(back, -1)
        got[n - step] = fore
        got[step] = back
    half = half_of(value.shape[1])
    left = shift(fore[:, :half], 1)
    right = shift(back[:, half:], -1)
    return [got[i] for i in range(n) if i != n // 2] + [left, right]


def ring_scatter(far, near):
    bf, f32 = jnp.bfloat16, jnp.float32
    rows = far.shape[0] // 3
    half = half_of(far.shape[1])
    part = {i: far[(i - 3) * rows : (i - 2) * rows] for i in (3, 4, 5)}
    left = shift(part[4][:, :half].astype(bf), 1)
    right = shift(part[4][:, half:].astype(bf), -1)
    fore = jnp.concatenate([part[3][:, :half] + left.astype(f32), part[3][:, half:]], axis=1).astype(bf)
    back = jnp.concatenate([part[5][:, :half], part[5][:, half:] + right.astype(f32)], axis=1).astype(bf)
    near = near((fore, back))
    part |= {i: near[j * rows : (j + 1) * rows] for j, i in enumerate((0, 1, 2, 6, 7))}
    for step in (2, 1):
        fore = (shift(fore, 1).astype(f32) + part[step]).astype(bf)
        back = (shift(back, -1).astype(f32) + part[8 - step]).astype(bf)
    fore = shift(fore, 1).astype(f32)
    back = shift(back, -1).astype(f32)
    return (part[0] + fore + back).astype(bf)


def row_gather(same, other, share, z):
    units = lax.axis_size("dp")
    rest = same.shape[1] - units * share
    half = half_of(rest)

    def slice_for(i):
        part = same if i % 2 == 0 else other
        return lax.dynamic_slice_in_dim(part, rest + (z + i) % 8 // 2 * share, share, axis=1)

    cat = lambda *v: jnp.concatenate(v, axis=1)
    four = slice_for(4)
    hs = share // 2
    x1, x0 = other[:, :rest], same[:, :rest]
    fore1 = shift(cat(x1, slice_for(1), slice_for(3)), 1)
    back1 = shift(cat(x1, slice_for(7), slice_for(5)), -1)
    fore2 = shift(cat(x0, slice_for(2), four[:, :hs]), 2)
    back2 = shift(cat(x0, slice_for(6), four[:, hs:]), -2)
    full = rest + share
    fore3 = shift(cat(fore1[:, :rest], fore1[:, full:]), 2)
    back3 = shift(cat(back1[:, :rest], back1[:, full:]), -2)
    left = shift(cat(fore2[:, :half], fore2[:, full:]), 2)
    right = shift(cat(back2[:, half:rest], back2[:, full:]), -2)
    far = cat(left[:, :half], right[:, :-hs], left[:, half:], right[:, -hs:])
    own = cat(x0, slice_for(0))
    return [own, back1[:, :full], back2[:, :full], back3, far, fore3, fore2[:, :full], fore1[:, :full]]


def row_scatter(parts):
    bf, f32 = jnp.bfloat16, jnp.float32
    half = half_of(parts[0].shape[1])
    add = lambda u, v: (u.astype(f32) + v.astype(f32)).astype(bf)
    fore3, back3 = shift(parts[3], 2), shift(parts[5], -2)
    left, right = shift(parts[4][:, :half], 2), shift(parts[4][:, half:], -2)
    two = jnp.concatenate([add(parts[2][:, :half], left), parts[2][:, half:]], axis=1)
    six = jnp.concatenate([parts[6][:, :half], add(parts[6][:, half:], right)], axis=1)
    one, seven = add(parts[1], fore3), add(parts[7], back3)
    fore1, back1 = shift(one, 1), shift(seven, -1)
    fore2, back2 = shift(two, 2), shift(six, -2)
    fore1, back1, fore2, back2 = lax.optimization_barrier((fore1, back1, fore2, back2))
    same = parts[0].astype(f32) + fore2.astype(f32) + back2.astype(f32)
    return same.astype(bf), add(fore1, back1)


def exchange(rows):
    n = lax.axis_size(PLANE)
    out = lax.all_to_all(rows.reshape(n, -1, rows.shape[1]), PLANE, 0, 0, tiled=True)
    return out.reshape(rows.shape)


def ranks(ids, own, rows):
    named = [ids[k][None, :] == own[:, None] for k in range(2)]
    member = (named[0] | named[1]).astype(jnp.bfloat16)
    before = (jnp.arange(rows)[:, None] < jnp.arange(rows)[None, :]).astype(jnp.bfloat16)
    rank = jnp.dot(member.reshape(-1, rows), before, preferred_element_type=jnp.float32)
    return named, rank.reshape(member.shape)


def own_slots(ids, own):
    named, rank = ranks(ids, own, ids.shape[1])
    hit = rank[:, None, :] == jnp.arange(8, dtype=jnp.float32)[None, :, None]
    return [
        (hit & named[k][:, None, :]).astype(jnp.bfloat16).reshape(-1, ids.shape[1])
        for k in range(2)
    ]


def dot(a, b):
    return jnp.dot(a, b, preferred_element_type=jnp.float32)


def dot_nt(a, b):
    return lax.dot_general(a, b, (((1,), (1,)), ((), ())), preferred_element_type=jnp.float32)


def dot_t(a, b):
    return lax.dot_general(a, b, (((0,), (0,)), ((), ())), preferred_element_type=jnp.float32)


def spread_kernel(own_ref, *refs):
    bf, f32 = jnp.bfloat16, jnp.float32
    *ids, id_left, left, right = refs[: 2 * 7 + 3]
    blocks, ids = ids[:7], ids[7:] + [id_left]
    out_ref, pick_ref, far_ref = refs[2 * 7 + 3 :]
    split = left.shape[1]
    tile = out_ref.shape[1]
    rows = own_ref.shape[1]
    at = (0, 1, 2, 3, 5, 6, 7, 4)
    step = pl.program_id(0)

    @pl.when(step == 0)
    def _():
        far_ref[:, :split] = left[...]
        far_ref[:, split:] = right[:, : far_ref.shape[1] - split]
        own = own_ref[...]
        before = lax.broadcasted_iota(jnp.int32, (rows, rows), 0) < lax.broadcasted_iota(jnp.int32, (rows, rows), 1)
        before = before.astype(f32).astype(bf)
        slot = lax.broadcasted_iota(jnp.int32, (8 * CAP, rows), 0)
        for i, ref in zip(at, ids):
            named = ref[...].astype(f32).T
            member = (named[0:1] == own) | (named[1:2] == own)
            rank = dot(member.astype(f32).astype(bf), before)
            rank = jnp.where(member, rank, -1.0)
            wanted = jnp.where(slot % 8 == i, slot // 8, -2).astype(f32)
            hit = rank[:, None, :] == wanted[None]
            hit = jnp.where(hit, 1.0, 0.0).reshape(-1, rows)
            pick_ref[:, i * rows : (i + 1) * rows] = hit.astype(bf)

    vals = {i: ref[...] for i, ref in zip(at, blocks)}
    vals[4] = far_ref[:, pl.ds(pl.multiple_of(step * tile, 128), tile)]
    vals = jnp.concatenate([vals[i] for i in range(8)], axis=0)
    out_ref[...] = dot(pick_ref[...], vals).astype(bf)


def spread(own, ring, cut):
    bf = jnp.bfloat16
    *blocks, left, right = ring
    rows = blocks[0].shape[0]
    tile = 768
    tail = (right.shape[1] - 128) // 128
    col = lambda f: pl.BlockSpec((rows, tile), lambda i: (0, f(i)))
    ids = lambda at: pl.BlockSpec((rows, 128), lambda i: (0, at))
    n = own.shape[0]
    whole = lambda v: pl.BlockSpec(v.shape, lambda i: (0, 0))
    return pl.pallas_call(
        spread_kernel,
        grid=(cut // tile,),
        in_specs=[pl.BlockSpec(own.shape, lambda i: (0, 0))]
        + [col(lambda i: i)] * 7
        + [ids(cut // 128)] * 7
        + [ids(tail), whole(left), whole(right)],
        out_specs=[
            pl.BlockSpec((n * 8 * CAP, tile), lambda i: (0, i)),
            pl.BlockSpec((n * 8 * CAP, 8 * rows), lambda i: (0, 0)),
        ],
        out_shape=[
            jax.ShapeDtypeStruct((n * 8 * CAP, cut), bf),
            jax.ShapeDtypeStruct((n * 8 * CAP, 8 * rows), bf),
        ],
        scratch_shapes=[pltpu.VMEM((rows, cut), bf)],
        compiler_params=pltpu.CompilerParams(vmem_limit_bytes=VMEM),
        cost_estimate=pl.CostEstimate(
            flops=2 * n * 8 * CAP * 8 * rows * cut, bytes_accessed=2 * n * 8 * CAP * 2 * cut, transcendentals=0
        ),
    )(own, *blocks, *blocks, right, left, right)


def grads_kernel(a_ref, b_ref, wg_ref, wu_ref, gate_ref, up_ref, back_ref):
    bf, f32 = jnp.bfloat16, jnp.float32
    cut = a_ref.shape[1]
    rest = wg_ref.shape[0] - cut
    gate_pre = dot(a_ref[...], wg_ref[:cut]) + dot(b_ref[:, :rest], wg_ref[cut:])
    up_pre = dot(a_ref[...], wu_ref[:cut]) + dot(b_ref[:, :rest], wu_ref[cut:])
    upstream = b_ref[:, rest:].astype(f32)
    sig = 1.0 / (1.0 + jnp.exp(-gate_pre))
    up_cot = (upstream * gate_pre * sig).astype(bf)
    gate_cot = (upstream * up_pre * sig * (1.0 + gate_pre * (1.0 - sig))).astype(bf)
    up_ref[...] = up_cot
    gate_ref[...] = gate_cot
    part = 256
    for lo in range(0, back_ref.shape[1], part):
        hi = min(lo + part, back_ref.shape[1])
        back_ref[:, lo:hi] = (dot_nt(gate_cot, wg_ref[lo:hi]) + dot_nt(up_cot, wu_ref[lo:hi])).astype(bf)


def local_grads(rows_a, rows_b, wg, wu, back):
    bf = jnp.bfloat16
    rows = rows_a.shape[0]
    width, share = wg.shape
    step = 256
    row = lambda n: pl.BlockSpec((step, n), lambda i: (i, 0))
    whole = pl.BlockSpec((width, share), lambda i: (0, 0))
    return pl.pallas_call(
        grads_kernel,
        grid=(rows // step,),
        in_specs=[row(rows_a.shape[1]), row(rows_b.shape[1]), whole, whole],
        out_specs=[row(share), row(share), row(back)],
        out_shape=[
            jax.ShapeDtypeStruct((rows, share), bf),
            jax.ShapeDtypeStruct((rows, share), bf),
            jax.ShapeDtypeStruct((rows, back), bf),
        ],
        compiler_params=pltpu.CompilerParams(vmem_limit_bytes=VMEM),
        cost_estimate=pl.CostEstimate(
            flops=4 * rows * share * (width + back), bytes_accessed=2 * rows * 2 * width, transcendentals=rows * share
        ),
    )(rows_a, rows_b, wg, wu)


def block_kernel(gate_ref, up_ref, wg_ref, wu_ref, *refs):
    bf, f32 = jnp.bfloat16, jnp.float32
    *out_refs, wide_ref = refs
    blocks = len(out_refs)
    rows, rest = out_refs[0].shape

    def by_block(c):
        c = c.astype(f32)
        for t in range(c.shape[1] // 128):
            wide_ref[t] = c[:, t * 128 : (t + 1) * 128]
        return jnp.concatenate(
            [
                jnp.concatenate([wide_ref[t, pl.ds(i, rows, stride=blocks), :] for t in range(c.shape[1] // 128)], axis=1)
                for i in range(blocks)
            ],
            axis=0,
        ).astype(bf)

    gate_cot, up_cot = by_block(gate_ref[...]), by_block(up_ref[...])
    part = 256
    for lo in range(0, rest, part):
        hi = min(lo + part, rest)
        wide = (dot_nt(gate_cot, wg_ref[lo:hi]) + dot_nt(up_cot, wu_ref[lo:hi])).astype(bf)
        for i in range(blocks):
            out_refs[i][:, lo:hi] = wide[i * rows : (i + 1) * rows]


def block_grads(gate_cot, up_cot, wg, wu):
    rows, share = gate_cot.shape
    rest = wg.shape[0]
    step = 256
    row = pl.BlockSpec((step, share), lambda i: (i, 0))
    whole = pl.BlockSpec((rest, share), lambda i: (0, 0))
    return pl.pallas_call(
        block_kernel,
        grid=(rows // step,),
        in_specs=[row, row, whole, whole],
        out_specs=[pl.BlockSpec((step // 8, rest), lambda i: (i, 0))] * 8,
        out_shape=[jax.ShapeDtypeStruct((rows // 8, rest), jnp.bfloat16)] * 8,
        scratch_shapes=[pltpu.VMEM((share // 128, step, 128), jnp.float32)],
        compiler_params=pltpu.CompilerParams(vmem_limit_bytes=24 * 2**20),
        cost_estimate=pl.CostEstimate(
            flops=4 * rows * share * rest, bytes_accessed=2 * rows * rest, transcendentals=0
        ),
    )(gate_cot, up_cot, wg, wu)


def on_device(tokens, routes, hidden_grad, w_gate, w_up):
    bf, f32 = jnp.bfloat16, jnp.float32
    blocks, n = lax.axis_size(RING), lax.axis_size(PLANE)
    zl, zh = lax.axis_index("zl"), lax.axis_index("dp")
    x = tokens[0]
    tok, width = x.shape
    cut = width * CUT // 28
    rest = width - cut
    wg, wu = w_gate[0], w_up[0]
    share = wg.shape[1]
    le = jnp.arange(n)
    plane = (le // 8) * 16 + le % 8
    pair = jnp.stack([zl, 1 - zl])

    ids = routes[0].T
    lanes = jnp.pad(routes[0].astype(bf), ((0, 0), (0, 126)))
    ring = ring_gather(jnp.concatenate([x[:, :cut], lanes], axis=1))

    own0, own1 = own_slots(ids, (plane[:, None] + 8 * pair[None, :]).reshape(-1))
    own = own0 + own1
    x_b, grads = x[:, cut:], hidden_grad[0]
    near = jnp.concatenate(
        [dot(own, x_b).astype(bf), (dot(own0, grads[:, 0]) + dot(own1, grads[:, 1])).astype(bf)],
        axis=1,
    )
    near = exchange(near)

    experts = jnp.broadcast_to((plane + zl * 8).astype(f32)[:, None], (n, tok))
    rows_a, pick = spread(experts, ring, cut)
    rows_a = exchange(rows_a)
    near = near.reshape(n, 2, 8, -1)[:, :, :CAP].transpose(1, 0, 2, 3).reshape(2, n * CAP, -1)
    got = row_gather(near[0], near[1], share, zh * 2 + zl)
    got = jnp.stack(got, axis=1).reshape(n * CAP * blocks, -1)
    rows_b = got[:, :rest]

    cut = width * CUT_BACK // 28
    rest = width - cut
    gate_cot, up_cot, back_a = local_grads(rows_a, got, wg, wu, cut)
    back_b = block_grads(gate_cot, up_cot, wg[cut:], wu[cut:])
    back_a = exchange(back_a)

    def weight_grad(c):
        return jnp.concatenate([dot_t(rows_a, c).astype(bf), dot_t(rows_b, c).astype(bf)], axis=0)

    grad_g, grad_u = weight_grad(gate_cot), weight_grad(up_cot)
    spot_far = pick[:, 3 * tok : 6 * tok].T
    spot_near = jnp.concatenate([pick[:, : 3 * tok], pick[:, 6 * tok :]], axis=1).T
    same, other = row_scatter(back_b)
    back_a, same, other, spot_far, spot_near = lax.optimization_barrier((back_a, same, other, spot_far, spot_near))

    grad_a = ring_scatter(
        dot(spot_far, back_a), lambda mark: dot(spot_near, lax.optimization_barrier((back_a, mark))[0])
    )
    back_b = jnp.stack([same.reshape(n, CAP, rest), other.reshape(n, CAP, rest)], axis=1)
    back_b = exchange(jnp.pad(back_b, ((0, 0), (0, 0), (0, 8 - CAP), (0, 0))).reshape(-1, rest))
    grad_b = dot_t(own, back_b).astype(bf)
    token_grad = jnp.concatenate([grad_a, grad_b], axis=1)
    return token_grad[None], grad_g[None], grad_u[None]


def solution(mesh):
    fine = Mesh(mesh.devices.reshape(4, 2, 4, 2, 4), ("x", "zl", "y", "core", "dp"))
    return jax.shard_map(
        on_device,
        mesh=fine,
        in_specs=(
            P("dp", EXPERT, None),
            P("dp", EXPERT, None),
            P("dp", EXPERT, None, None),
            P(EXPERT, None, "dp"),
            P(EXPERT, None, "dp"),
        ),
        out_specs=(P("dp", EXPERT, None), P(EXPERT, None, "dp"), P(EXPERT, None, "dp")),
        check_vma=False,
    )
```

```python
import functools

import jax
import jax.numpy as jnp
from jax import lax
from jax.experimental import pallas as pl
from jax.experimental.pallas import tpu as pltpu
from jax.sharding import Mesh, PartitionSpec as P

RING = ("zl", "dp")
PLANE = ("x", "y", "core")
EXPERT = ("x", "zl", "y", "core")
CAP = 5
VMEM = 56 * 2**20
CUT = 18
CUT_BACK = 18


def shift(value, step):
    n, far = lax.axis_size(RING), lax.axis_size("dp")
    at = [(z % 2) * far + z // 2 for z in range(n)]
    return lax.ppermute(value, RING, [(at[z], at[(z + step) % n]) for z in range(n)])


def half_of(width):
    return (width // 256 + 1) // 2 * 256


def ring_gather(value):
    n = lax.axis_size(RING)
    got = {0: value}
    fore = back = value
    for step in range(1, n // 2):
        fore = shift(fore, 1)
        back = shift(back, -1)
        got[n - step] = fore
        got[step] = back
    half = half_of(value.shape[1])
    left = shift(fore[:, :half], 1)
    right = shift(back[:, half:], -1)
    return [got[i] for i in range(n) if i != n // 2] + [left, right]


def ring_scatter(far, near):
    bf, f32 = jnp.bfloat16, jnp.float32
    rows = far.shape[0] // 3
    half = half_of(far.shape[1])
    part = {i: far[(i - 3) * rows : (i - 2) * rows] for i in (3, 4, 5)}
    left = shift(part[4][:, :half].astype(bf), 1)
    right = shift(part[4][:, half:].astype(bf), -1)
    fore = jnp.concatenate([part[3][:, :half] + left.astype(f32), part[3][:, half:]], axis=1).astype(bf)
    back = jnp.concatenate([part[5][:, :half], part[5][:, half:] + right.astype(f32)], axis=1).astype(bf)
    near = near((fore, back))
    part |= {i: near[j * rows : (j + 1) * rows] for j, i in enumerate((0, 1, 2, 6, 7))}
    for step in (2, 1):
        fore = (shift(fore, 1).astype(f32) + part[step]).astype(bf)
        back = (shift(back, -1).astype(f32) + part[8 - step]).astype(bf)
    fore = shift(fore, 1).astype(f32)
    back = shift(back, -1).astype(f32)
    return (part[0] + fore + back).astype(bf)


def row_gather(same, other, share, z):
    units = lax.axis_size("dp")
    rest = same.shape[1] - units * share
    half = half_of(rest)

    def slice_for(i):
        part = same if i % 2 == 0 else other
        return lax.dynamic_slice_in_dim(part, rest + (z + i) % 8 // 2 * share, share, axis=1)

    cat = lambda *v: jnp.concatenate(v, axis=1)
    four = slice_for(4)
    hs = share // 2
    x1, x0 = other[:, :rest], same[:, :rest]
    fore1 = shift(cat(x1, slice_for(1), slice_for(3)), 1)
    back1 = shift(cat(x1, slice_for(7), slice_for(5)), -1)
    fore2 = shift(cat(x0, slice_for(2), four[:, :hs]), 2)
    back2 = shift(cat(x0, slice_for(6), four[:, hs:]), -2)
    full = rest + share
    fore3 = shift(cat(fore1[:, :rest], fore1[:, full:]), 2)
    back3 = shift(cat(back1[:, :rest], back1[:, full:]), -2)
    left = shift(cat(fore2[:, :half], fore2[:, full:]), 2)
    right = shift(cat(back2[:, half:rest], back2[:, full:]), -2)
    far = cat(left[:, :half], right[:, :-hs], left[:, half:], right[:, -hs:])
    own = cat(x0, slice_for(0))
    return [own, back1[:, :full], back2[:, :full], back3, far, fore3, fore2[:, :full], fore1[:, :full]]


def row_scatter(parts):
    bf, f32 = jnp.bfloat16, jnp.float32
    half = half_of(parts[0].shape[1])
    add = lambda u, v: (u.astype(f32) + v.astype(f32)).astype(bf)
    fore3, back3 = shift(parts[3], 2), shift(parts[5], -2)
    left, right = shift(parts[4][:, :half], 2), shift(parts[4][:, half:], -2)
    two = jnp.concatenate([add(parts[2][:, :half], left), parts[2][:, half:]], axis=1)
    six = jnp.concatenate([parts[6][:, :half], add(parts[6][:, half:], right)], axis=1)
    fore3, back3 = lax.optimization_barrier((fore3, back3))
    one, seven = add(parts[1], fore3), add(parts[7], back3)
    fore1, back1 = shift(one, 1), shift(seven, -1)
    fore2, back2 = shift(two, 2), shift(six, -2)
    fore1, back1, fore2, back2 = lax.optimization_barrier((fore1, back1, fore2, back2))
    same = parts[0].astype(f32) + fore2.astype(f32) + back2.astype(f32)
    return same.astype(bf), add(fore1, back1), (fore3, back3)


def exchange(rows):
    n = lax.axis_size(PLANE)
    out = lax.all_to_all(rows.reshape(n, -1, rows.shape[1]), PLANE, 0, 0, tiled=True)
    return out.reshape(rows.shape)


def ranks(ids, own, rows):
    named = [ids[k][None, :] == own[:, None] for k in range(2)]
    member = (named[0] | named[1]).astype(jnp.bfloat16)
    before = (jnp.arange(rows)[:, None] < jnp.arange(rows)[None, :]).astype(jnp.bfloat16)
    rank = jnp.dot(member.reshape(-1, rows), before, preferred_element_type=jnp.float32)
    return named, rank.reshape(member.shape)


def own_slots(ids, own):
    named, rank = ranks(ids, own, ids.shape[1])
    hit = rank[:, None, :] == jnp.arange(8, dtype=jnp.float32)[None, :, None]
    return [
        (hit & named[k][:, None, :]).astype(jnp.bfloat16).reshape(-1, ids.shape[1])
        for k in range(2)
    ]


def dot(a, b):
    return jnp.dot(a, b, preferred_element_type=jnp.float32)


def dot_nt(a, b):
    return lax.dot_general(a, b, (((1,), (1,)), ((), ())), preferred_element_type=jnp.float32)


def dot_t(a, b):
    return lax.dot_general(a, b, (((0,), (0,)), ((), ())), preferred_element_type=jnp.float32)


def spread_kernel(own_ref, *refs):
    bf, f32 = jnp.bfloat16, jnp.float32
    *ids, id_left, left, right = refs[: 2 * 7 + 3]
    blocks, ids = ids[:7], ids[7:] + [id_left]
    out_ref, pick_ref, far_ref = refs[2 * 7 + 3 :]
    split = left.shape[1]
    tile = out_ref.shape[1]
    rows = own_ref.shape[1]
    at = (0, 1, 2, 3, 5, 6, 7, 4)
    step = pl.program_id(0)

    @pl.when(step == 0)
    def _():
        far_ref[:, :split] = left[...]
        far_ref[:, split:] = right[:, : far_ref.shape[1] - split]
        own = own_ref[...]
        before = lax.broadcasted_iota(jnp.int32, (rows, rows), 0) < lax.broadcasted_iota(jnp.int32, (rows, rows), 1)
        before = before.astype(f32).astype(bf)
        slot = lax.broadcasted_iota(jnp.int32, (8 * CAP, rows), 0)
        for i, ref in zip(at, ids):
            named = ref[...].astype(f32).T
            member = (named[0:1] == own) | (named[1:2] == own)
            rank = dot(member.astype(f32).astype(bf), before)
            rank = jnp.where(member, rank, -1.0)
            wanted = jnp.where(slot % 8 == i, slot // 8, -2).astype(f32)
            hit = rank[:, None, :] == wanted[None]
            hit = jnp.where(hit, 1.0, 0.0).reshape(-1, rows)
            pick_ref[:, i * rows : (i + 1) * rows] = hit.astype(bf)

    vals = {i: ref[...] for i, ref in zip(at, blocks)}
    vals[4] = far_ref[:, pl.ds(pl.multiple_of(step * tile, 128), tile)]
    vals = jnp.concatenate([vals[i] for i in range(8)], axis=0)
    out_ref[...] = dot(pick_ref[...], vals).astype(bf)


def spread(own, ring, cut):
    bf = jnp.bfloat16
    *blocks, left, right = ring
    rows = blocks[0].shape[0]
    tile = 768
    tail = (right.shape[1] - 128) // 128
    col = lambda f: pl.BlockSpec((rows, tile), lambda i: (0, f(i)))
    ids = lambda at: pl.BlockSpec((rows, 128), lambda i: (0, at))
    n = own.shape[0]
    whole = lambda v: pl.BlockSpec(v.shape, lambda i: (0, 0))
    return pl.pallas_call(
        spread_kernel,
        grid=(cut // tile,),
        in_specs=[pl.BlockSpec(own.shape, lambda i: (0, 0))]
        + [col(lambda i: i)] * 7
        + [ids(cut // 128)] * 7
        + [ids(tail), whole(left), whole(right)],
        out_specs=[
            pl.BlockSpec((n * 8 * CAP, tile), lambda i: (0, i)),
            pl.BlockSpec((n * 8 * CAP, 8 * rows), lambda i: (0, 0)),
        ],
        out_shape=[
            jax.ShapeDtypeStruct((n * 8 * CAP, cut), bf),
            jax.ShapeDtypeStruct((n * 8 * CAP, 8 * rows), bf),
        ],
        scratch_shapes=[pltpu.VMEM((rows, cut), bf)],
        compiler_params=pltpu.CompilerParams(vmem_limit_bytes=VMEM),
        cost_estimate=pl.CostEstimate(
            flops=2 * n * 8 * CAP * 8 * rows * cut, bytes_accessed=2 * n * 8 * CAP * 2 * cut, transcendentals=0
        ),
    )(own, *blocks, *blocks, right, left, right)


def grads_kernel(a_ref, b_ref, wg_ref, wu_ref, gate_ref, up_ref, back_ref):
    bf, f32 = jnp.bfloat16, jnp.float32
    cut = a_ref.shape[1]
    rest = wg_ref.shape[0] - cut
    gate_pre = dot(a_ref[...], wg_ref[:cut]) + dot(b_ref[:, :rest], wg_ref[cut:])
    up_pre = dot(a_ref[...], wu_ref[:cut]) + dot(b_ref[:, :rest], wu_ref[cut:])
    upstream = b_ref[:, rest:].astype(f32)
    sig = 1.0 / (1.0 + jnp.exp(-gate_pre))
    up_cot = (upstream * gate_pre * sig).astype(bf)
    gate_cot = (upstream * up_pre * sig * (1.0 + gate_pre * (1.0 - sig))).astype(bf)
    up_ref[...] = up_cot
    gate_ref[...] = gate_cot
    part = 256
    for lo in range(0, back_ref.shape[1], part):
        hi = min(lo + part, back_ref.shape[1])
        back_ref[:, lo:hi] = (dot_nt(gate_cot, wg_ref[lo:hi]) + dot_nt(up_cot, wu_ref[lo:hi])).astype(bf)


def local_grads(rows_a, rows_b, wg, wu, back):
    bf = jnp.bfloat16
    rows = rows_a.shape[0]
    width, share = wg.shape
    step = 256
    row = lambda n: pl.BlockSpec((step, n), lambda i: (i, 0))
    whole = pl.BlockSpec((width, share), lambda i: (0, 0))
    return pl.pallas_call(
        grads_kernel,
        grid=(rows // step,),
        in_specs=[row(rows_a.shape[1]), row(rows_b.shape[1]), whole, whole],
        out_specs=[row(share), row(share), row(back)],
        out_shape=[
            jax.ShapeDtypeStruct((rows, share), bf),
            jax.ShapeDtypeStruct((rows, share), bf),
            jax.ShapeDtypeStruct((rows, back), bf),
        ],
        compiler_params=pltpu.CompilerParams(vmem_limit_bytes=VMEM),
        cost_estimate=pl.CostEstimate(
            flops=4 * rows * share * (width + back), bytes_accessed=2 * rows * 2 * width, transcendentals=rows * share
        ),
    )(rows_a, rows_b, wg, wu)


def block_kernel(gate_ref, up_ref, wg_ref, wu_ref, *refs):
    bf, f32 = jnp.bfloat16, jnp.float32
    *out_refs, wide_ref = refs
    blocks = len(out_refs)
    rows, rest = out_refs[0].shape

    def by_block(c):
        c = c.astype(f32)
        for t in range(c.shape[1] // 128):
            wide_ref[t] = c[:, t * 128 : (t + 1) * 128]
        return jnp.concatenate(
            [
                jnp.concatenate([wide_ref[t, pl.ds(i, rows, stride=blocks), :] for t in range(c.shape[1] // 128)], axis=1)
                for i in range(blocks)
            ],
            axis=0,
        ).astype(bf)

    gate_cot, up_cot = by_block(gate_ref[...]), by_block(up_ref[...])
    part = 256
    for lo in range(0, rest, part):
        hi = min(lo + part, rest)
        wide = (dot_nt(gate_cot, wg_ref[lo:hi]) + dot_nt(up_cot, wu_ref[lo:hi])).astype(bf)
        for i in range(blocks):
            out_refs[i][:, lo:hi] = wide[i * rows : (i + 1) * rows]


def block_grads(gate_cot, up_cot, wg, wu):
    rows, share = gate_cot.shape
    rest = wg.shape[0]
    step = 256
    row = pl.BlockSpec((step, share), lambda i: (i, 0))
    whole = pl.BlockSpec((rest, share), lambda i: (0, 0))
    return pl.pallas_call(
        block_kernel,
        grid=(rows // step,),
        in_specs=[row, row, whole, whole],
        out_specs=[pl.BlockSpec((step // 8, rest), lambda i: (i, 0))] * 8,
        out_shape=[jax.ShapeDtypeStruct((rows // 8, rest), jnp.bfloat16)] * 8,
        scratch_shapes=[pltpu.VMEM((share // 128, step, 128), jnp.float32)],
        compiler_params=pltpu.CompilerParams(vmem_limit_bytes=24 * 2**20),
        cost_estimate=pl.CostEstimate(
            flops=4 * rows * share * rest, bytes_accessed=2 * rows * rest, transcendentals=0
        ),
    )(gate_cot, up_cot, wg, wu)


def weights_kernel(split, a_ref, b_ref, gate_ref, up_ref, grad_gate_ref, grad_up_ref, cots_ref):
    bf, f32 = jnp.bfloat16, jnp.float32
    share = gate_ref.shape[1]
    step = pl.program_id(0)

    @pl.when(step == 0)
    def _():
        cots_ref[:share] = gate_ref[...].T
        cots_ref[share:] = up_ref[...].T

    def write(rows):
        both = dot(cots_ref[...], rows)
        grad_gate_ref[...] = both[:share].T.astype(bf)
        grad_up_ref[...] = both[share:].T.astype(bf)

    @pl.when(step < split)
    def _():
        write(a_ref[...])

    @pl.when(step >= split)
    def _():
        write(b_ref[...])


def weight_grads(rows_a, rows_b, gate_cot, up_cot):
    bf = jnp.bfloat16
    rows, cut = rows_a.shape
    share = gate_cot.shape[1]
    width = cut + rows_b.shape[1] - share
    tile = 256
    split = cut // tile
    whole = pl.BlockSpec((rows, share), lambda i: (0, 0))
    return pl.pallas_call(
        functools.partial(weights_kernel, split),
        grid=(width // tile,),
        in_specs=[
            pl.BlockSpec((rows, tile), lambda i: (0, jnp.minimum(i, split - 1))),
            pl.BlockSpec((rows, tile), lambda i: (0, jnp.maximum(i - split, 0))),
            whole,
            whole,
        ],
        out_specs=[pl.BlockSpec((tile, share), lambda i: (i, 0))] * 2,
        out_shape=[jax.ShapeDtypeStruct((width, share), bf)] * 2,
        scratch_shapes=[pltpu.VMEM((2 * share, rows), bf)],
        compiler_params=pltpu.CompilerParams(vmem_limit_bytes=24 * 2**20),
        cost_estimate=pl.CostEstimate(flops=0, bytes_accessed=0, transcendentals=0),
    )(rows_a, rows_b, gate_cot, up_cot)


def on_device(tokens, routes, hidden_grad, w_gate, w_up):
    bf, f32 = jnp.bfloat16, jnp.float32
    blocks, n = lax.axis_size(RING), lax.axis_size(PLANE)
    zl, zh = lax.axis_index("zl"), lax.axis_index("dp")
    x = tokens[0]
    tok, width = x.shape
    cut = width * CUT // 28
    rest = width - cut
    wg, wu = w_gate[0], w_up[0]
    share = wg.shape[1]
    le = jnp.arange(n)
    plane = (le // 8) * 16 + le % 8
    pair = jnp.stack([zl, 1 - zl])

    ids = routes[0].T
    lanes = jnp.pad(routes[0].astype(bf), ((0, 0), (0, 126)))
    ring = ring_gather(jnp.concatenate([x[:, :cut], lanes], axis=1))

    own0, own1 = own_slots(ids, (plane[:, None] + 8 * pair[None, :]).reshape(-1))
    own = own0 + own1
    x_b, grads = x[:, cut:], hidden_grad[0]
    near = jnp.concatenate(
        [dot(own, x_b).astype(bf), (dot(own0, grads[:, 0]) + dot(own1, grads[:, 1])).astype(bf)],
        axis=1,
    )
    near = exchange(near)

    experts = jnp.broadcast_to((plane + zl * 8).astype(f32)[:, None], (n, tok))
    rows_a, pick = spread(experts, ring, cut)
    rows_a = exchange(rows_a)
    near = near.reshape(n, 2, 8, -1)[:, :, :CAP].transpose(1, 0, 2, 3).reshape(2, n * CAP, -1)
    got = row_gather(near[0], near[1], share, zh * 2 + zl)
    got = jnp.stack(got, axis=1).reshape(n * CAP * blocks, -1)

    cut = width * CUT_BACK // 28
    rest = width - cut
    gate_cot, up_cot, back_a = local_grads(rows_a, got, wg, wu, cut)
    back_b = block_grads(gate_cot, up_cot, wg[cut:], wu[cut:])
    back_a = exchange(back_a)

    same, other, mark = row_scatter(back_b)
    gate_cot, up_cot, pick, mark = lax.optimization_barrier((gate_cot, up_cot, pick, mark))
    grad_g, grad_u = weight_grads(rows_a, got, gate_cot, up_cot)
    spot_far = pick[:, 3 * tok : 6 * tok].T
    spot_near = jnp.concatenate([pick[:, : 3 * tok], pick[:, 6 * tok :]], axis=1).T
    back_a, same, other, spot_far, spot_near, grad_g, grad_u = lax.optimization_barrier(
        (back_a, same, other, spot_far, spot_near, grad_g, grad_u)
    )

    grad_a = ring_scatter(
        dot(spot_far, back_a), lambda mark: dot(spot_near, lax.optimization_barrier((back_a, mark))[0])
    )
    back_b = jnp.stack([same.reshape(n, CAP, rest), other.reshape(n, CAP, rest)], axis=1)
    back_b = exchange(jnp.pad(back_b, ((0, 0), (0, 0), (0, 8 - CAP), (0, 0))).reshape(-1, rest))
    grad_b = dot_t(own, back_b).astype(bf)
    token_grad = jnp.concatenate([grad_a, grad_b], axis=1)
    return token_grad[None], grad_g[None], grad_u[None]


def solution(mesh):
    fine = Mesh(mesh.devices.reshape(4, 2, 4, 2, 4), ("x", "zl", "y", "core", "dp"))
    return jax.shard_map(
        on_device,
        mesh=fine,
        in_specs=(
            P("dp", EXPERT, None),
            P("dp", EXPERT, None),
            P("dp", EXPERT, None, None),
            P(EXPERT, None, "dp"),
            P(EXPERT, None, "dp"),
        ),
        out_specs=(P("dp", EXPERT, None), P(EXPERT, None, "dp"), P(EXPERT, None, "dp")),
        check_vma=False,
    )
```

```python
import functools

import jax
import jax.numpy as jnp
from jax import lax
from jax.experimental import pallas as pl
from jax.experimental.pallas import tpu as pltpu
from jax.sharding import Mesh, PartitionSpec as P

RING = ("zl", "dp")
PLANE = ("x", "y", "core")
EXPERT = ("x", "zl", "y", "core")
CAP = 5
VMEM = 56 * 2**20
CUT = 16
CUT_BACK = 17


def shift(value, step):
    n, far = lax.axis_size(RING), lax.axis_size("dp")
    at = [(z % 2) * far + z // 2 for z in range(n)]
    return lax.ppermute(value, RING, [(at[z], at[(z + step) % n]) for z in range(n)])


def half_of(width):
    return (width // 256 + 1) // 2 * 256


def ring_gather(value):
    n = lax.axis_size(RING)
    got = {0: value}
    fore = back = value
    for step in range(1, n // 2):
        fore = shift(fore, 1)
        back = shift(back, -1)
        got[n - step] = fore
        got[step] = back
    half = half_of(value.shape[1])
    left = shift(fore[:, :half], 1)
    right = shift(back[:, half:], -1)
    return [got[i] for i in range(n) if i != n // 2] + [left, right]


def ring_scatter(far, near):
    bf, f32 = jnp.bfloat16, jnp.float32
    rows = far.shape[0] // 3
    half = half_of(far.shape[1])
    part = {i: far[(i - 3) * rows : (i - 2) * rows] for i in (3, 4, 5)}
    left = shift(part[4][:, :half].astype(bf), 1)
    right = shift(part[4][:, half:].astype(bf), -1)
    fore = jnp.concatenate([part[3][:, :half] + left.astype(f32), part[3][:, half:]], axis=1).astype(bf)
    back = jnp.concatenate([part[5][:, :half], part[5][:, half:] + right.astype(f32)], axis=1).astype(bf)
    near = near((fore, back))
    part |= {i: near[j * rows : (j + 1) * rows] for j, i in enumerate((0, 1, 2, 6, 7))}
    for step in (2, 1):
        fore = (shift(fore, 1).astype(f32) + part[step]).astype(bf)
        back = (shift(back, -1).astype(f32) + part[8 - step]).astype(bf)
    fore = shift(fore, 1).astype(f32)
    back = shift(back, -1).astype(f32)
    return (part[0] + fore + back).astype(bf)


def row_gather(same, other, share, z):
    units = lax.axis_size("dp")
    rest = same.shape[1] - units * share
    half = half_of(rest)

    def slice_for(i):
        part = same if i % 2 == 0 else other
        return lax.dynamic_slice_in_dim(part, rest + (z + i) % 8 // 2 * share, share, axis=1)

    cat = lambda *v: jnp.concatenate(v, axis=1)
    four = slice_for(4)
    hs = share // 2
    x1, x0 = other[:, :rest], same[:, :rest]
    fore1 = shift(cat(x1, slice_for(1), slice_for(3)), 1)
    back1 = shift(cat(x1, slice_for(7), slice_for(5)), -1)
    fore2 = shift(cat(x0, slice_for(2), four[:, :hs]), 2)
    back2 = shift(cat(x0, slice_for(6), four[:, hs:]), -2)
    full = rest + share
    fore3 = shift(cat(fore1[:, :rest], fore1[:, full:]), 2)
    back3 = shift(cat(back1[:, :rest], back1[:, full:]), -2)
    left = shift(cat(fore2[:, :half], fore2[:, full:]), 2)
    right = shift(cat(back2[:, half:rest], back2[:, full:]), -2)
    far = cat(left[:, :half], right[:, :-hs], left[:, half:], right[:, -hs:])
    own = cat(x0, slice_for(0))
    return [own, back1, back2, back3, far, fore3, fore2, fore1]


def row_scatter(parts):
    bf, f32 = jnp.bfloat16, jnp.float32
    half = half_of(parts[0].shape[1])
    add = lambda u, v: (u.astype(f32) + v.astype(f32)).astype(bf)
    fore3, back3 = shift(parts[3], 2), shift(parts[5], -2)
    left, right = shift(parts[4][:, :half], 2), shift(parts[4][:, half:], -2)
    two = jnp.concatenate([add(parts[2][:, :half], left), parts[2][:, half:]], axis=1)
    six = jnp.concatenate([parts[6][:, :half], add(parts[6][:, half:], right)], axis=1)
    fore3, back3 = lax.optimization_barrier((fore3, back3))
    one, seven = add(parts[1], fore3), add(parts[7], back3)
    fore1, back1 = shift(one, 1), shift(seven, -1)
    fore2, back2 = shift(two, 2), shift(six, -2)
    fore1, back1, fore2, back2 = lax.optimization_barrier((fore1, back1, fore2, back2))
    same = parts[0].astype(f32) + fore2.astype(f32) + back2.astype(f32)
    return same.astype(bf), add(fore1, back1), (fore3, back3)


def exchange(rows):
    n = lax.axis_size(PLANE)
    out = lax.all_to_all(rows.reshape(n, -1, rows.shape[1]), PLANE, 0, 0, tiled=True)
    return out.reshape(rows.shape)


def ranks(ids, own, rows):
    named = [ids[k][None, :] == own[:, None] for k in range(2)]
    member = (named[0] | named[1]).astype(jnp.bfloat16)
    before = (jnp.arange(rows)[:, None] < jnp.arange(rows)[None, :]).astype(jnp.bfloat16)
    rank = jnp.dot(member.reshape(-1, rows), before, preferred_element_type=jnp.float32)
    return named, rank.reshape(member.shape)


def own_slots(ids, own):
    named, rank = ranks(ids, own, ids.shape[1])
    hit = rank[:, None, :] == jnp.arange(8, dtype=jnp.float32)[None, :, None]
    return [
        (hit & named[k][:, None, :]).astype(jnp.bfloat16).reshape(-1, ids.shape[1])
        for k in range(2)
    ]


def dot(a, b):
    return jnp.dot(a, b, preferred_element_type=jnp.float32)


def dot_nt(a, b):
    return lax.dot_general(a, b, (((1,), (1,)), ((), ())), preferred_element_type=jnp.float32)


def dot_t(a, b):
    return lax.dot_general(a, b, (((0,), (0,)), ((), ())), preferred_element_type=jnp.float32)


def spread_kernel(own_ref, *refs):
    bf, f32 = jnp.bfloat16, jnp.float32
    *ids, id_left, left, right = refs[: 2 * 7 + 3]
    blocks, ids = ids[:7], ids[7:] + [id_left]
    out_ref, pick_ref, far_ref = refs[2 * 7 + 3 :]
    split = left.shape[1]
    tile = out_ref.shape[1]
    rows = own_ref.shape[1]
    at = (0, 1, 2, 3, 5, 6, 7, 4)
    step = pl.program_id(0)

    @pl.when(step == 0)
    def _():
        far_ref[:, :split] = left[...]
        far_ref[:, split:] = right[:, : far_ref.shape[1] - split]
        own = own_ref[...]
        before = lax.broadcasted_iota(jnp.int32, (rows, rows), 0) < lax.broadcasted_iota(jnp.int32, (rows, rows), 1)
        before = before.astype(f32).astype(bf)
        slot = lax.broadcasted_iota(jnp.int32, (8 * CAP, rows), 0)
        for i, ref in zip(at, ids):
            named = ref[...].astype(f32).T
            member = (named[0:1] == own) | (named[1:2] == own)
            rank = dot(member.astype(f32).astype(bf), before)
            rank = jnp.where(member, rank, -1.0)
            wanted = jnp.where(slot % 8 == i, slot // 8, -2).astype(f32)
            hit = rank[:, None, :] == wanted[None]
            hit = jnp.where(hit, 1.0, 0.0).reshape(-1, rows)
            pick_ref[:, i * rows : (i + 1) * rows] = hit.astype(bf)

    vals = {i: ref[...] for i, ref in zip(at, blocks)}
    vals[4] = far_ref[:, pl.ds(pl.multiple_of(step * tile, 128), tile)]
    vals = jnp.concatenate([vals[i] for i in range(8)], axis=0)
    out_ref[...] = dot(pick_ref[...], vals).astype(bf)


def spread(own, ring, cut):
    bf = jnp.bfloat16
    *blocks, left, right = ring
    rows = blocks[0].shape[0]
    tile = 1024
    tail = (right.shape[1] - 128) // 128
    col = lambda f: pl.BlockSpec((rows, tile), lambda i: (0, f(i)))
    ids = lambda at: pl.BlockSpec((rows, 128), lambda i: (0, at))
    n = own.shape[0]
    whole = lambda v: pl.BlockSpec(v.shape, lambda i: (0, 0))
    return pl.pallas_call(
        spread_kernel,
        grid=(cut // tile,),
        in_specs=[pl.BlockSpec(own.shape, lambda i: (0, 0))]
        + [col(lambda i: i)] * 7
        + [ids(cut // 128)] * 7
        + [ids(tail), whole(left), whole(right)],
        out_specs=[
            pl.BlockSpec((n * 8 * CAP, tile), lambda i: (0, i)),
            pl.BlockSpec((n * 8 * CAP, 8 * rows), lambda i: (0, 0)),
        ],
        out_shape=[
            jax.ShapeDtypeStruct((n * 8 * CAP, cut), bf),
            jax.ShapeDtypeStruct((n * 8 * CAP, 8 * rows), bf),
        ],
        scratch_shapes=[pltpu.VMEM((rows, cut), bf)],
        compiler_params=pltpu.CompilerParams(vmem_limit_bytes=VMEM),
        cost_estimate=pl.CostEstimate(
            flops=2 * n * 8 * CAP * 8 * rows * cut, bytes_accessed=2 * n * 8 * CAP * 2 * cut, transcendentals=0
        ),
    )(own, *blocks, *blocks, right, left, right)


def grads_kernel(a_ref, *refs):
    bf, f32 = jnp.bfloat16, jnp.float32
    *b_refs, wg_ref, wu_ref, gate_ref, up_ref, back_ref, wide_ref = refs
    cut = a_ref.shape[1]
    rest = wg_ref.shape[0] - cut
    blocks = len(b_refs)
    rows = a_ref.shape[0] // blocks
    by_block = jnp.concatenate([b[...] for b in b_refs], axis=0)
    x_b = by_block[:, :rest]

    def in_order(c):
        for t in range(c.shape[1] // 128):
            for i in range(blocks):
                wide_ref[t, pl.ds(i, rows, stride=blocks), :] = c[i * rows : (i + 1) * rows, t * 128 : (t + 1) * 128]
        return jnp.concatenate([wide_ref[t] for t in range(c.shape[1] // 128)], axis=1)

    upstream = in_order(by_block[:, rest:].astype(f32))
    gate_pre = dot(a_ref[...], wg_ref[:cut]) + in_order(dot(x_b, wg_ref[cut:]))
    up_pre = dot(a_ref[...], wu_ref[:cut]) + in_order(dot(x_b, wu_ref[cut:]))
    sig = 1.0 / (1.0 + jnp.exp(-gate_pre))
    up_cot = (upstream * gate_pre * sig).astype(bf)
    gate_cot = (upstream * up_pre * sig * (1.0 + gate_pre * (1.0 - sig))).astype(bf)
    up_ref[...] = up_cot
    gate_ref[...] = gate_cot
    part = 256
    for lo in range(0, back_ref.shape[1], part):
        hi = min(lo + part, back_ref.shape[1])
        back_ref[:, lo:hi] = (dot_nt(gate_cot, wg_ref[lo:hi]) + dot_nt(up_cot, wu_ref[lo:hi])).astype(bf)


def local_grads(rows_a, rows_b, wg, wu, back):
    bf = jnp.bfloat16
    rows = rows_a.shape[0]
    width, share = wg.shape
    step = 256
    rest = width - rows_a.shape[1] + share
    row = lambda n: pl.BlockSpec((step, n), lambda i: (i, 0))
    whole = pl.BlockSpec((width, share), lambda i: (0, 0))
    return pl.pallas_call(
        grads_kernel,
        grid=(rows // step,),
        in_specs=[row(rows_a.shape[1])] + [pl.BlockSpec((step // 8, rest), lambda i: (i, 0))] * 8 + [whole, whole],
        out_specs=[row(share), row(share), row(back)],
        out_shape=[
            jax.ShapeDtypeStruct((rows, share), bf),
            jax.ShapeDtypeStruct((rows, share), bf),
            jax.ShapeDtypeStruct((rows, back), bf),
        ],
        scratch_shapes=[pltpu.VMEM((share // 128, step, 128), jnp.float32)],
        compiler_params=pltpu.CompilerParams(vmem_limit_bytes=VMEM),
        cost_estimate=pl.CostEstimate(
            flops=4 * rows * share * (width + back), bytes_accessed=2 * rows * 2 * width, transcendentals=rows * share
        ),
    )(rows_a, *rows_b, wg, wu)


def block_kernel(gate_ref, up_ref, wg_ref, wu_ref, *refs):
    bf, f32 = jnp.bfloat16, jnp.float32
    *out_refs, gate_out_ref, up_out_ref, wide_ref = refs
    blocks = len(out_refs)
    rows, rest = out_refs[0].shape

    def by_block(c):
        c = c.astype(f32)
        for t in range(c.shape[1] // 128):
            wide_ref[t] = c[:, t * 128 : (t + 1) * 128]
        return jnp.concatenate(
            [
                jnp.concatenate([wide_ref[t, pl.ds(i, rows, stride=blocks), :] for t in range(c.shape[1] // 128)], axis=1)
                for i in range(blocks)
            ],
            axis=0,
        ).astype(bf)

    gate_cot, up_cot = by_block(gate_ref[...]), by_block(up_ref[...])
    gate_out_ref[...] = gate_cot.reshape(gate_out_ref.shape)
    up_out_ref[...] = up_cot.reshape(up_out_ref.shape)
    part = 256
    for lo in range(0, rest, part):
        hi = min(lo + part, rest)
        wide = (dot_nt(gate_cot, wg_ref[lo:hi]) + dot_nt(up_cot, wu_ref[lo:hi])).astype(bf)
        for i in range(blocks):
            out_refs[i][:, lo:hi] = wide[i * rows : (i + 1) * rows]


def block_grads(gate_cot, up_cot, wg, wu):
    rows, share = gate_cot.shape
    rest = wg.shape[0]
    step = 256
    row = pl.BlockSpec((step, share), lambda i: (i, 0))
    whole = pl.BlockSpec((rest, share), lambda i: (0, 0))
    return pl.pallas_call(
        block_kernel,
        grid=(rows // step,),
        in_specs=[row, row, whole, whole],
        out_specs=[pl.BlockSpec((step // 8, rest), lambda i: (i, 0))] * 8
        + [pl.BlockSpec((8, step // 8, share), lambda i: (0, i, 0))] * 2,
        out_shape=[jax.ShapeDtypeStruct((rows // 8, rest), jnp.bfloat16)] * 8
        + [jax.ShapeDtypeStruct((8, rows // 8, share), jnp.bfloat16)] * 2,
        scratch_shapes=[pltpu.VMEM((share // 128, step, 128), jnp.float32)],
        compiler_params=pltpu.CompilerParams(vmem_limit_bytes=24 * 2**20),
        cost_estimate=pl.CostEstimate(
            flops=4 * rows * share * rest, bytes_accessed=2 * rows * rest, transcendentals=0
        ),
    )(gate_cot, up_cot, wg, wu)


def weights_kernel(split, a_ref, *refs):
    bf, f32 = jnp.bfloat16, jnp.float32
    *b_refs, gate_ref, up_ref, gate_by_ref, up_by_ref, grad_gate_ref, grad_up_ref, cots_ref = refs
    rows, share = gate_ref.shape
    step = pl.program_id(0)

    @pl.when(step == 0)
    def _():
        cots_ref[0, :share] = gate_ref[...].T
        cots_ref[0, share:] = up_ref[...].T
        cots_ref[1, :share] = gate_by_ref[...].reshape(rows, share).T
        cots_ref[1, share:] = up_by_ref[...].reshape(rows, share).T

    def write(cots, rows):
        both = dot(cots, rows)
        grad_gate_ref[...] = both[:share].T.astype(bf)
        grad_up_ref[...] = both[share:].T.astype(bf)

    @pl.when(step < split)
    def _():
        write(cots_ref[0], a_ref[...])

    @pl.when(step >= split)
    def _():
        write(cots_ref[1], jnp.concatenate([b[...] for b in b_refs], axis=0))


def weight_grads(rows_a, rows_b, gate_cot, up_cot, gate_by, up_by, width):
    bf = jnp.bfloat16
    rows, cut = rows_a.shape
    share = gate_cot.shape[1]
    tile = 256
    split = cut // tile
    whole = pl.BlockSpec((rows, share), lambda i: (0, 0))
    return pl.pallas_call(
        functools.partial(weights_kernel, split),
        grid=(width // tile,),
        in_specs=[
            pl.BlockSpec((rows, tile), lambda i: (0, jnp.minimum(i, split - 1))),
            *[pl.BlockSpec((rows // 8, tile), lambda i: (0, jnp.maximum(i - split, 0)))] * 8,
            whole,
            whole,
            *[pl.BlockSpec((8, rows // 8, share), lambda i: (0, 0, 0))] * 2,
        ],
        out_specs=[pl.BlockSpec((tile, share), lambda i: (i, 0))] * 2,
        out_shape=[jax.ShapeDtypeStruct((width, share), bf)] * 2,
        scratch_shapes=[pltpu.VMEM((2, 2 * share, rows), bf)],
        compiler_params=pltpu.CompilerParams(vmem_limit_bytes=24 * 2**20),
        cost_estimate=pl.CostEstimate(flops=0, bytes_accessed=0, transcendentals=0),
    )(rows_a, *rows_b, gate_cot, up_cot, gate_by, up_by)


def on_device(tokens, routes, hidden_grad, w_gate, w_up):
    bf, f32 = jnp.bfloat16, jnp.float32
    blocks, n = lax.axis_size(RING), lax.axis_size(PLANE)
    zl, zh = lax.axis_index("zl"), lax.axis_index("dp")
    x = tokens[0]
    tok, width = x.shape
    cut = width * CUT // 28
    rest = width - cut
    wg, wu = w_gate[0], w_up[0]
    share = wg.shape[1]
    le = jnp.arange(n)
    plane = (le // 8) * 16 + le % 8
    pair = jnp.stack([zl, 1 - zl])

    ids = routes[0].T
    lanes = jnp.pad(routes[0].astype(bf), ((0, 0), (0, 126)))
    ring = ring_gather(jnp.concatenate([x[:, :cut], lanes], axis=1))

    own0, own1 = own_slots(ids, (plane[:, None] + 8 * pair[None, :]).reshape(-1))
    own = own0 + own1
    x_b, grads = x[:, cut:], hidden_grad[0]
    near = jnp.concatenate(
        [dot(own, x_b).astype(bf), (dot(own0, grads[:, 0]) + dot(own1, grads[:, 1])).astype(bf)],
        axis=1,
    )
    near = exchange(near)

    experts = jnp.broadcast_to((plane + zl * 8).astype(f32)[:, None], (n, tok))
    rows_a, pick = spread(experts, ring, cut)
    rows_a = exchange(rows_a)
    near = near.reshape(n, 2, 8, -1)[:, :, :CAP].transpose(1, 0, 2, 3).reshape(2, n * CAP, -1)
    got = row_gather(near[0], near[1], share, zh * 2 + zl)

    cut = width * CUT_BACK // 28
    rest = width - cut
    gate_cot, up_cot, back_a = local_grads(rows_a, got, wg, wu, cut)
    *back_b, gate_by, up_by = block_grads(gate_cot, up_cot, wg[cut:], wu[cut:])
    back_a = exchange(back_a)

    same, other, mark = row_scatter(back_b)
    gate_cot, up_cot, pick, mark = lax.optimization_barrier((gate_cot, up_cot, pick, mark))
    grad_g, grad_u = weight_grads(rows_a, got, gate_cot, up_cot, gate_by, up_by, width)
    spot_far = pick[:, 3 * tok : 6 * tok].T
    spot_near = jnp.concatenate([pick[:, : 3 * tok], pick[:, 6 * tok :]], axis=1).T
    back_a, same, other, spot_far, spot_near, grad_g, grad_u = lax.optimization_barrier(
        (back_a, same, other, spot_far, spot_near, grad_g, grad_u)
    )

    grad_a = ring_scatter(
        dot(spot_far, back_a), lambda mark: dot(spot_near, lax.optimization_barrier((back_a, mark))[0])
    )
    back_b = jnp.stack([same.reshape(n, CAP, rest), other.reshape(n, CAP, rest)], axis=1)
    back_b = exchange(jnp.pad(back_b, ((0, 0), (0, 0), (0, 8 - CAP), (0, 0))).reshape(-1, rest))
    grad_b = dot_t(own, back_b).astype(bf)
    token_grad = jnp.concatenate([grad_a, grad_b], axis=1)
    return token_grad[None], grad_g[None], grad_u[None]


def solution(mesh):
    fine = Mesh(mesh.devices.reshape(4, 2, 4, 2, 4), ("x", "zl", "y", "core", "dp"))
    return jax.shard_map(
        on_device,
        mesh=fine,
        in_specs=(
            P("dp", EXPERT, None),
            P("dp", EXPERT, None),
            P("dp", EXPERT, None, None),
            P(EXPERT, None, "dp"),
            P(EXPERT, None, "dp"),
        ),
        out_specs=(P("dp", EXPERT, None), P(EXPERT, None, "dp"), P(EXPERT, None, "dp")),
        check_vma=False,
    )
```

```python
import jax
import jax.numpy as jnp
from jax import lax
from jax.experimental import pallas as pl
from jax.experimental.pallas import tpu as pltpu
from jax.sharding import Mesh, PartitionSpec as P

RING = ("zl", "dp")
PLANE = ("x", "y", "core")
EXPERT = ("x", "zl", "y", "core")
CAP = 5
VMEM = 56 * 2**20
CUT = 18
CUT_BACK = 17


def shift(value, step):
    n, far = lax.axis_size(RING), lax.axis_size("dp")
    at = [(z % 2) * far + z // 2 for z in range(n)]
    return lax.ppermute(value, RING, [(at[z], at[(z + step) % n]) for z in range(n)])


def half_of(width):
    return (width // 256 + 1) // 2 * 256


def ring_gather(value):
    n = lax.axis_size(RING)
    got = {0: value}
    fore = back = value
    for step in range(1, n // 2):
        fore = shift(fore, 1)
        back = shift(back, -1)
        got[n - step] = fore
        got[step] = back
    half = half_of(value.shape[1])
    left = shift(fore[:, :half], 1)
    right = shift(back[:, half:], -1)
    return [got[i] for i in range(n) if i != n // 2] + [left, right]


def ring_scatter(far, near):
    bf, f32 = jnp.bfloat16, jnp.float32
    rows = far.shape[0] // 3
    half = half_of(far.shape[1])
    part = {i: far[(i - 3) * rows : (i - 2) * rows] for i in (3, 4, 5)}
    left = shift(part[4][:, :half].astype(bf), 1)
    right = shift(part[4][:, half:].astype(bf), -1)
    fore = jnp.concatenate([part[3][:, :half] + left.astype(f32), part[3][:, half:]], axis=1).astype(bf)
    back = jnp.concatenate([part[5][:, :half], part[5][:, half:] + right.astype(f32)], axis=1).astype(bf)
    near = near((fore, back))
    part |= {i: near[j * rows : (j + 1) * rows] for j, i in enumerate((0, 1, 2, 6, 7))}
    for step in (2, 1):
        fore = (shift(fore, 1).astype(f32) + part[step]).astype(bf)
        back = (shift(back, -1).astype(f32) + part[8 - step]).astype(bf)
    fore = shift(fore, 1).astype(f32)
    back = shift(back, -1).astype(f32)
    return (part[0] + fore + back).astype(bf)


def row_gather(same, other, share, z):
    units = lax.axis_size("dp")
    rest = same.shape[1] - units * share
    half = half_of(rest)

    def slice_for(i):
        part = same if i % 2 == 0 else other
        return lax.dynamic_slice_in_dim(part, rest + (z + i) % 8 // 2 * share, share, axis=1)

    cat = lambda *v: jnp.concatenate(v, axis=1)
    four = slice_for(4)
    hs = share // 2
    x1, x0 = other[:, :rest], same[:, :rest]
    fore1 = shift(cat(x1, slice_for(1), slice_for(3)), 1)
    back1 = shift(cat(x1, slice_for(7), slice_for(5)), -1)
    fore2 = shift(cat(x0, slice_for(2), four[:, :hs]), 2)
    back2 = shift(cat(x0, slice_for(6), four[:, hs:]), -2)
    full = rest + share
    fore3 = shift(cat(fore1[:, :rest], fore1[:, full:]), 2)
    back3 = shift(cat(back1[:, :rest], back1[:, full:]), -2)
    left = shift(cat(fore2[:, :half], fore2[:, full:]), 2)
    right = shift(cat(back2[:, half:rest], back2[:, full:]), -2)
    far = cat(left[:, :half], right[:, :-hs], left[:, half:], right[:, -hs:])
    own = cat(x0, slice_for(0))
    return [own, back1[:, :full], back2[:, :full], back3, far, fore3, fore2[:, :full], fore1[:, :full]]


def row_scatter(parts):
    bf, f32 = jnp.bfloat16, jnp.float32
    half = half_of(parts[0].shape[1])
    add = lambda u, v: (u.astype(f32) + v.astype(f32)).astype(bf)
    fore3, back3 = shift(parts[3], 2), shift(parts[5], -2)
    left, right = shift(parts[4][:, :half], 2), shift(parts[4][:, half:], -2)
    two = jnp.concatenate([add(parts[2][:, :half], left), parts[2][:, half:]], axis=1)
    six = jnp.concatenate([parts[6][:, :half], add(parts[6][:, half:], right)], axis=1)
    fore3, back3 = lax.optimization_barrier((fore3, back3))
    one, seven = add(parts[1], fore3), add(parts[7], back3)
    fore1, back1 = shift(one, 1), shift(seven, -1)
    fore2, back2 = shift(two, 2), shift(six, -2)
    fore1, back1, fore2, back2 = lax.optimization_barrier((fore1, back1, fore2, back2))
    same = parts[0].astype(f32) + fore2.astype(f32) + back2.astype(f32)
    return same.astype(bf), add(fore1, back1)


def exchange(rows):
    n = lax.axis_size(PLANE)
    out = lax.all_to_all(rows.reshape(n, -1, rows.shape[1]), PLANE, 0, 0, tiled=True)
    return out.reshape(rows.shape)


def ranks(ids, own, rows):
    named = [ids[k][None, :] == own[:, None] for k in range(2)]
    member = (named[0] | named[1]).astype(jnp.bfloat16)
    before = (jnp.arange(rows)[:, None] < jnp.arange(rows)[None, :]).astype(jnp.bfloat16)
    rank = jnp.dot(member.reshape(-1, rows), before, preferred_element_type=jnp.float32)
    return named, rank.reshape(member.shape)


def own_slots(ids, own):
    named, rank = ranks(ids, own, ids.shape[1])
    hit = rank[:, None, :] == jnp.arange(8, dtype=jnp.float32)[None, :, None]
    return [
        (hit & named[k][:, None, :]).astype(jnp.bfloat16).reshape(-1, ids.shape[1])
        for k in range(2)
    ]


def dot(a, b):
    return jnp.dot(a, b, preferred_element_type=jnp.float32)


def dot_nt(a, b):
    return lax.dot_general(a, b, (((1,), (1,)), ((), ())), preferred_element_type=jnp.float32)


def dot_t(a, b):
    return lax.dot_general(a, b, (((0,), (0,)), ((), ())), preferred_element_type=jnp.float32)


def spread_kernel(own_ref, *refs):
    bf, f32 = jnp.bfloat16, jnp.float32
    *ids, id_left, left, right = refs[: 2 * 7 + 3]
    blocks, ids = ids[:7], ids[7:] + [id_left]
    out_ref, pick_ref, far_ref = refs[2 * 7 + 3 :]
    split = left.shape[1]
    tile = out_ref.shape[1]
    rows = own_ref.shape[1]
    at = (0, 1, 2, 3, 5, 6, 7, 4)
    step = pl.program_id(0)

    @pl.when(step == 0)
    def _():
        far_ref[:, :split] = left[...]
        far_ref[:, split:] = right[:, : far_ref.shape[1] - split]
        own = own_ref[...]
        before = lax.broadcasted_iota(jnp.int32, (rows, rows), 0) < lax.broadcasted_iota(jnp.int32, (rows, rows), 1)
        before = before.astype(f32).astype(bf)
        slot = lax.broadcasted_iota(jnp.int32, (8 * CAP, rows), 0)
        for i, ref in zip(at, ids):
            named = ref[...].astype(f32).T
            member = (named[0:1] == own) | (named[1:2] == own)
            rank = dot(member.astype(f32).astype(bf), before)
            rank = jnp.where(member, rank, -1.0)
            wanted = jnp.where(slot % 8 == i, slot // 8, -2).astype(f32)
            hit = rank[:, None, :] == wanted[None]
            hit = jnp.where(hit, 1.0, 0.0).reshape(-1, rows)
            pick_ref[:, i * rows : (i + 1) * rows] = hit.astype(bf)

    vals = {i: ref[...] for i, ref in zip(at, blocks)}
    vals[4] = far_ref[:, pl.ds(pl.multiple_of(step * tile, 128), tile)]
    vals = jnp.concatenate([vals[i] for i in range(8)], axis=0)
    out_ref[...] = dot(pick_ref[...], vals).astype(bf)


def spread(own, ring, cut):
    bf = jnp.bfloat16
    *blocks, left, right = ring
    rows = blocks[0].shape[0]
    tile = 768
    tail = (right.shape[1] - 128) // 128
    col = lambda f: pl.BlockSpec((rows, tile), lambda i: (0, f(i)))
    ids = lambda at: pl.BlockSpec((rows, 128), lambda i: (0, at))
    n = own.shape[0]
    whole = lambda v: pl.BlockSpec(v.shape, lambda i: (0, 0))
    return pl.pallas_call(
        spread_kernel,
        grid=(cut // tile,),
        in_specs=[pl.BlockSpec(own.shape, lambda i: (0, 0))]
        + [col(lambda i: i)] * 7
        + [ids(cut // 128)] * 7
        + [ids(tail), whole(left), whole(right)],
        out_specs=[
            pl.BlockSpec((n * 8 * CAP, tile), lambda i: (0, i)),
            pl.BlockSpec((n * 8 * CAP, 8 * rows), lambda i: (0, 0)),
        ],
        out_shape=[
            jax.ShapeDtypeStruct((n * 8 * CAP, cut), bf),
            jax.ShapeDtypeStruct((n * 8 * CAP, 8 * rows), bf),
        ],
        scratch_shapes=[pltpu.VMEM((rows, cut), bf)],
        compiler_params=pltpu.CompilerParams(vmem_limit_bytes=VMEM),
        cost_estimate=pl.CostEstimate(
            flops=2 * n * 8 * CAP * 8 * rows * cut, bytes_accessed=2 * n * 8 * CAP * 2 * cut, transcendentals=0
        ),
    )(own, *blocks, *blocks, right, left, right)


def grads_kernel(a_ref, b_ref, wg_ref, wu_ref, gate_ref, up_ref, back_ref):
    bf, f32 = jnp.bfloat16, jnp.float32
    cut = a_ref.shape[1]
    rest = wg_ref.shape[0] - cut
    gate_pre = dot(a_ref[...], wg_ref[:cut]) + dot(b_ref[:, :rest], wg_ref[cut:])
    up_pre = dot(a_ref[...], wu_ref[:cut]) + dot(b_ref[:, :rest], wu_ref[cut:])
    upstream = b_ref[:, rest:].astype(f32)
    sig = 1.0 / (1.0 + jnp.exp(-gate_pre))
    up_cot = (upstream * gate_pre * sig).astype(bf)
    gate_cot = (upstream * up_pre * sig * (1.0 + gate_pre * (1.0 - sig))).astype(bf)
    up_ref[...] = up_cot
    gate_ref[...] = gate_cot
    part = 256
    for lo in range(0, back_ref.shape[1], part):
        hi = min(lo + part, back_ref.shape[1])
        back_ref[:, lo:hi] = (dot_nt(gate_cot, wg_ref[lo:hi]) + dot_nt(up_cot, wu_ref[lo:hi])).astype(bf)


def local_grads(rows_a, rows_b, wg, wu, back):
    bf = jnp.bfloat16
    rows = rows_a.shape[0]
    width, share = wg.shape
    step = 256
    row = lambda n: pl.BlockSpec((step, n), lambda i: (i, 0))
    whole = pl.BlockSpec((width, share), lambda i: (0, 0))
    return pl.pallas_call(
        grads_kernel,
        grid=(rows // step,),
        in_specs=[row(rows_a.shape[1]), row(rows_b.shape[1]), whole, whole],
        out_specs=[row(share), row(share), row(back)],
        out_shape=[
            jax.ShapeDtypeStruct((rows, share), bf),
            jax.ShapeDtypeStruct((rows, share), bf),
            jax.ShapeDtypeStruct((rows, back), bf),
        ],
        compiler_params=pltpu.CompilerParams(vmem_limit_bytes=VMEM),
        cost_estimate=pl.CostEstimate(
            flops=4 * rows * share * (width + back), bytes_accessed=2 * rows * 2 * width, transcendentals=rows * share
        ),
    )(rows_a, rows_b, wg, wu)


def block_kernel(gate_ref, up_ref, wg_ref, wu_ref, *refs):
    bf, f32 = jnp.bfloat16, jnp.float32
    *out_refs, wide_ref = refs
    blocks = len(out_refs)
    rows, rest = out_refs[0].shape

    def by_block(c):
        c = c.astype(f32)
        for t in range(c.shape[1] // 128):
            wide_ref[t] = c[:, t * 128 : (t + 1) * 128]
        return jnp.concatenate(
            [
                jnp.concatenate([wide_ref[t, pl.ds(i, rows, stride=blocks), :] for t in range(c.shape[1] // 128)], axis=1)
                for i in range(blocks)
            ],
            axis=0,
        ).astype(bf)

    gate_cot, up_cot = by_block(gate_ref[...]), by_block(up_ref[...])
    part = 256
    for lo in range(0, rest, part):
        hi = min(lo + part, rest)
        wide = (dot_nt(gate_cot, wg_ref[lo:hi]) + dot_nt(up_cot, wu_ref[lo:hi])).astype(bf)
        for i in range(blocks):
            out_refs[i][:, lo:hi] = wide[i * rows : (i + 1) * rows]


def block_grads(gate_cot, up_cot, wg, wu):
    rows, share = gate_cot.shape
    rest = wg.shape[0]
    step = 256
    row = pl.BlockSpec((step, share), lambda i: (i, 0))
    whole = pl.BlockSpec((rest, share), lambda i: (0, 0))
    return pl.pallas_call(
        block_kernel,
        grid=(rows // step,),
        in_specs=[row, row, whole, whole],
        out_specs=[pl.BlockSpec((step // 8, rest), lambda i: (i, 0))] * 8,
        out_shape=[jax.ShapeDtypeStruct((rows // 8, rest), jnp.bfloat16)] * 8,
        scratch_shapes=[pltpu.VMEM((share // 128, step, 128), jnp.float32)],
        compiler_params=pltpu.CompilerParams(vmem_limit_bytes=24 * 2**20),
        cost_estimate=pl.CostEstimate(
            flops=4 * rows * share * rest, bytes_accessed=2 * rows * rest, transcendentals=0
        ),
    )(gate_cot, up_cot, wg, wu)


def on_device(tokens, routes, hidden_grad, w_gate, w_up):
    bf, f32 = jnp.bfloat16, jnp.float32
    blocks, n = lax.axis_size(RING), lax.axis_size(PLANE)
    zl, zh = lax.axis_index("zl"), lax.axis_index("dp")
    x = tokens[0]
    tok, width = x.shape
    cut = width * CUT // 28
    rest = width - cut
    wg, wu = w_gate[0], w_up[0]
    share = wg.shape[1]
    le = jnp.arange(n)
    plane = (le // 8) * 16 + le % 8
    pair = jnp.stack([zl, 1 - zl])

    ids = routes[0].T
    lanes = jnp.pad(routes[0].astype(bf), ((0, 0), (0, 126)))
    ring = ring_gather(jnp.concatenate([x[:, :cut], lanes], axis=1))

    own0, own1 = own_slots(ids, (plane[:, None] + 8 * pair[None, :]).reshape(-1))
    own = own0 + own1
    x_b, grads = x[:, cut:], hidden_grad[0]
    near = jnp.concatenate(
        [dot(own, x_b).astype(bf), (dot(own0, grads[:, 0]) + dot(own1, grads[:, 1])).astype(bf)],
        axis=1,
    )
    near = exchange(near)

    experts = jnp.broadcast_to((plane + zl * 8).astype(f32)[:, None], (n, tok))
    rows_a, pick = spread(experts, ring, cut)
    rows_a = exchange(rows_a)
    near = near.reshape(n, 2, 8, -1)[:, :, :CAP].transpose(1, 0, 2, 3).reshape(2, n * CAP, -1)
    got = row_gather(near[0], near[1], share, zh * 2 + zl)
    got = jnp.stack(got, axis=1).reshape(n * CAP * blocks, -1)
    rows_b = got[:, :rest]

    cut = width * CUT_BACK // 28
    rest = width - cut
    gate_cot, up_cot, back_a = local_grads(rows_a, got, wg, wu, cut)
    back_b = block_grads(gate_cot, up_cot, wg[cut:], wu[cut:])
    back_a = exchange(back_a)

    def weight_grad(c):
        return jnp.concatenate([dot_t(rows_a, c).astype(bf), dot_t(rows_b, c).astype(bf)], axis=0)

    grad_g, grad_u = weight_grad(gate_cot), weight_grad(up_cot)
    spot_far = pick[:, 3 * tok : 6 * tok].T
    spot_near = jnp.concatenate([pick[:, : 3 * tok], pick[:, 6 * tok :]], axis=1).T
    same, other = row_scatter(back_b)
    back_a, same, other, spot_far, spot_near = lax.optimization_barrier((back_a, same, other, spot_far, spot_near))

    grad_a = ring_scatter(
        dot(spot_far, back_a), lambda mark: dot(spot_near, lax.optimization_barrier((back_a, mark))[0])
    )
    back_b = jnp.stack([same.reshape(n, CAP, rest), other.reshape(n, CAP, rest)], axis=1)
    back_b = exchange(jnp.pad(back_b, ((0, 0), (0, 0), (0, 8 - CAP), (0, 0))).reshape(-1, rest))
    grad_b = dot_t(own, back_b).astype(bf)
    token_grad = jnp.concatenate([grad_a, grad_b], axis=1)
    return token_grad[None], grad_g[None], grad_u[None]


def solution(mesh):
    fine = Mesh(mesh.devices.reshape(4, 2, 4, 2, 4), ("x", "zl", "y", "core", "dp"))
    return jax.shard_map(
        on_device,
        mesh=fine,
        in_specs=(
            P("dp", EXPERT, None),
            P("dp", EXPERT, None),
            P("dp", EXPERT, None, None),
            P(EXPERT, None, "dp"),
            P(EXPERT, None, "dp"),
        ),
        out_specs=(P("dp", EXPERT, None), P(EXPERT, None, "dp"), P(EXPERT, None, "dp")),
        check_vma=False,
    )
```
